256 devices in a mesh: roll: 32 (over y, z_hi, x), head: 8 (over z_lo, core).
Axes of the slice: x: 4, y: 4, z: 8 (z_hi: 2, z_lo: 4; z = z_hi * 4 + z_lo), core: 2. Of those that a mesh axis runs over, the one named last changes fastest.
Arguments:
- queries: bfloat16 [8192, 8192], P(('roll', 'head')), may hold values from -130 to 130
- keys: bfloat16 [8192, 1024], P(('roll', 'head')), may hold values from -7 to 7
- values: bfloat16 [8192, 1024], P(('roll', 'head')), may hold values from -6 to 6
- cotangent: bfloat16 [8192, 8192], P(('roll', 'head')), may hold values from -6 to 6
- doc_keys: bfloat16 [8192, 1024], P('roll', 'head'), may hold values from -6 to 6
- doc_values: bfloat16 [8192, 1024], P('roll', 'head'), may hold values from -6 to 6
- citations: int32 [32, 16], replicated, may hold values from 0 to 63, as said below
- block_lists: int32 [64, 4], P('roll'), may hold values from 0 to 15, as said below
Outputs:
- attended: bfloat16 [8192, 8192], P(('roll', 'head'))
- query_grad: bfloat16 [8192, 8192], P(('roll', 'head'))
- key_grad: bfloat16 [8192, 1024], P(('roll', 'head'))
- value_grad: bfloat16 [8192, 1024], P(('roll', 'head'))
- doc_key_grad: float32 [8192, 1024], P('roll', 'head')
- doc_value_grad: float32 [8192, 1024], P('roll', 'head')
The draws below stay inside these ranges and needn't reach their ends.
Inputs may be any that keep to these rules, and one draw needn't show every extreme that they name: `citations`: each row names 16 documents of 16 different owners; document d belongs to roll index d // 2. `block_lists`: each row names 4 different positions.
All inputs are finite; a program needn't handle non-finite values.
Results may differ from the reference program's by a relative error of at most 0.015.
Values may be sent and summed in bfloat16 or wider, within the bound.
A program may use at most 64 MiB of HBM per device.

```python
import math
import jax
import jax.numpy as jnp
from jax import lax

HD = 128
QH = 64
KVH = 8
BLOCK = 128
QTOK = 256
LIST = 4
CITE = 16
DOC_DEV = 2
ROLLS = 32
TOKENS = 8192
DOCS = 64
QBLOCKS = 2


def shared_keys(key):
    return jnp.clip(jax.random.normal(key, (TOKENS, KVH * HD), jnp.float32), -6.0, 6.0)


def draw_keys(key, part):
    base = shared_keys(key)
    return base.astype(jnp.bfloat16)


def draw_queries(key, part):
    key = jax.random.fold_in(key, 5)
    fresh = jnp.clip(jax.random.normal(key, (TOKENS, QH * HD), jnp.float32), -6.0, 6.0)
    return fresh.astype(jnp.bfloat16)


def draw_citations(key, part):
    key = jax.random.fold_in(key, 7)
    first, second, third = jax.random.split(key, 3)
    ranked = jax.random.randint(first, (ROLLS, ROLLS), 0, 1 << 20) * ROLLS + jnp.arange(ROLLS, dtype=jnp.int32)[None, :]
    owners = jnp.argsort(ranked, axis=1)[:, :CITE]
    spread_pick = jax.random.randint(second, (ROLLS, CITE), 0, 4) == 0
    other_doc = jax.random.randint(third, (ROLLS, CITE), 0, DOC_DEV)
    local_doc = jnp.where(spread_pick, other_doc, 0)
    return (owners * DOC_DEV + local_doc).astype(jnp.int32)


def draw_block_lists(key, part):
    key = jax.random.fold_in(key, 9)
    ranked = jax.random.randint(key, (ROLLS * QBLOCKS, CITE), 0, 1 << 20) * CITE + jnp.arange(CITE, dtype=jnp.int32)[None, :]
    return jnp.argsort(ranked, axis=1)[:, :LIST].astype(jnp.int32)


def block_levels(stream_key, shape, cuts, smallest, top_value):
    loudness = 1.0
    for position, parts in cuts:
        heights = jax.random.uniform(jax.random.fold_in(jax.random.fold_in(stream_key, 6), position), (parts,), jnp.float32, smallest / len(cuts), top_value / len(cuts))
        loudness = loudness * jnp.repeat(jnp.exp(heights), shape[position] // parts).reshape((-1,) + (1,) * (len(shape) - 1 - position))
    return loudness


def scatter_about(stream_key, shape, scale, limit, cuts=(), kind=jnp.bfloat16):
    array = scale * jax.random.normal(stream_key, shape, jnp.float32)
    if cuts:
        array = array * block_levels(stream_key, shape, cuts, -0.22, 0.18)
    return jnp.clip(array, -limit, limit).astype(kind)


def setup_inputs(seed: int = 0) -> dict:
    streams_of = jax.random.split(jax.random.key(seed), 9)
    return {
        "queries": draw_queries(jax.random.fold_in(streams_of[8], 71), 0),
        "keys": draw_keys(jax.random.fold_in(streams_of[8], 71), 0),
        "values": scatter_about(streams_of[2], (TOKENS, KVH * HD), 1.0, 6.0, ((0, 256),)),
        "cotangent": scatter_about(streams_of[3], (TOKENS, QH * HD), 1.0, 6.0, ((0, 256),)),
        "doc_keys": scatter_about(streams_of[4], (DOCS * BLOCK, KVH * HD), 1.0, 6.0, ((0, 32), (1, 8))),
        "doc_values": scatter_about(streams_of[5], (DOCS * BLOCK, KVH * HD), 1.0, 6.0, ((0, 32), (1, 8))),
        "citations": draw_citations(jax.random.fold_in(streams_of[8], 71), 0),
        "block_lists": draw_block_lists(jax.random.fold_in(streams_of[8], 71), 0),
    }


def block_pass(query, grad_out, key_loc, value_loc, key_doc, value_doc, start):
    f = jnp.float32
    scale = 1.0 / math.sqrt(query.shape[-1])
    query_f = query.astype(f)
    grad_f = grad_out.astype(f)
    key_loc_f = key_loc.astype(f)
    value_loc_f = value_loc.astype(f)
    key_doc_f = key_doc.astype(f)
    value_doc_f = value_doc.astype(f)
    score_loc = jnp.einsum('igqd,jgd->gqij', query_f, key_loc_f) * scale
    rows_pos = start + jnp.arange(query.shape[0], dtype=jnp.int32)
    cols_pos = jnp.arange(key_loc.shape[0], dtype=jnp.int32)
    visible = cols_pos[None, :] <= rows_pos[:, None]
    score_loc = jnp.where(visible, score_loc, -jnp.inf)
    score_doc = jnp.einsum('igqd,jgd->gqij', query_f, key_doc_f) * scale
    top = jnp.maximum(lax.optimization_barrier(jnp.max(score_loc, axis=-1)), lax.optimization_barrier(jnp.max(score_doc, axis=-1)))[..., None]
    exp_loc = jnp.exp(score_loc - top)
    exp_doc = jnp.exp(score_doc - top)
    total = lax.optimization_barrier(jnp.sum(exp_loc, axis=-1, keepdims=True)) + lax.optimization_barrier(jnp.sum(exp_doc, axis=-1, keepdims=True))
    prob_loc = exp_loc / total
    prob_doc = exp_doc / total
    weight_loc = prob_loc.astype(jnp.bfloat16).astype(f)
    weight_doc = prob_doc.astype(jnp.bfloat16).astype(f)
    output = jnp.einsum('gqij,jgd->igqd', weight_loc, value_loc_f) + jnp.einsum('gqij,jgd->igqd', weight_doc, value_doc_f)
    dprob_loc = jnp.einsum('igqd,jgd->gqij', grad_f, value_loc_f)
    dprob_doc = jnp.einsum('igqd,jgd->gqij', grad_f, value_doc_f)
    delta = lax.optimization_barrier(jnp.sum(prob_loc * dprob_loc, axis=-1, keepdims=True)) + lax.optimization_barrier(jnp.sum(prob_doc * dprob_doc, axis=-1, keepdims=True))
    dscore_loc = (prob_loc * (dprob_loc - delta)).astype(jnp.bfloat16).astype(f)
    dscore_doc = (prob_doc * (dprob_doc - delta)).astype(jnp.bfloat16).astype(f)
    dquery = (jnp.einsum('gqij,jgd->igqd', dscore_loc, key_loc_f) + jnp.einsum('gqij,jgd->igqd', dscore_doc, key_doc_f)) * scale
    dkey_loc = jnp.einsum('gqij,igqd->jgd', dscore_loc, query_f) * scale
    dvalue_loc = jnp.einsum('gqij,igqd->jgd', weight_loc, grad_f)
    dkey_doc = jnp.einsum('gqij,igqd->jgd', dscore_doc, query_f) * scale
    dvalue_doc = jnp.einsum('gqij,igqd->jgd', weight_doc, grad_f)
    return (output.astype(jnp.bfloat16), dquery.astype(jnp.bfloat16), dkey_loc, dvalue_loc, dkey_doc, dvalue_doc)

def reference(queries, keys, values, cotangent, doc_keys, doc_values, citations, block_lists):
    group = QH // KVH
    query_all = queries.reshape(ROLLS, QBLOCKS, BLOCK, KVH, group, HD)
    grad_all = cotangent.reshape(ROLLS, QBLOCKS, BLOCK, KVH, group, HD)
    key_all = keys.reshape(ROLLS, QTOK, KVH, HD)
    value_all = values.reshape(ROLLS, QTOK, KVH, HD)
    doc_key_all = doc_keys.reshape(DOCS, BLOCK, KVH, HD)
    doc_value_all = doc_values.reshape(DOCS, BLOCK, KVH, HD)
    lists = block_lists.reshape(ROLLS, QBLOCKS, LIST)
    listed = jax.vmap(lambda cites, rows: cites[rows])(citations, lists).astype(jnp.int32)

    def one_rollout(carry, item):
        query_r, grad_r, key_r, value_r, ids_r = item
        outputs = []
        dqueries = []
        dkey_docs = []
        dvalue_docs = []
        key_acc = jnp.zeros((QTOK, KVH, HD), jnp.float32)
        value_acc = jnp.zeros((QTOK, KVH, HD), jnp.float32)
        for index_b in range(QBLOCKS):
            end = (index_b + 1) * BLOCK
            key_doc = doc_key_all[ids_r[index_b]].reshape(LIST * BLOCK, KVH, HD)
            value_doc = doc_value_all[ids_r[index_b]].reshape(LIST * BLOCK, KVH, HD)
            output, dquery, dkey_loc, dvalue_loc, dkey_doc, dvalue_doc = block_pass(query_r[index_b], grad_r[index_b], key_r[:end], value_r[:end], key_doc, value_doc, index_b * BLOCK)
            key_acc = key_acc.at[:end].add(dkey_loc)
            value_acc = value_acc.at[:end].add(dvalue_loc)
            outputs.append(output)
            dqueries.append(dquery)
            dkey_docs.append(dkey_doc)
            dvalue_docs.append(dvalue_doc)
        sum_key, sum_value = carry
        flat_ids = ids_r.reshape(-1)
        sum_key = sum_key.at[flat_ids].add(jnp.stack(dkey_docs).reshape(QBLOCKS * LIST, BLOCK, KVH, HD))
        sum_value = sum_value.at[flat_ids].add(jnp.stack(dvalue_docs).reshape(QBLOCKS * LIST, BLOCK, KVH, HD))
        return ((sum_key, sum_value), (jnp.stack(outputs), jnp.stack(dqueries), key_acc, value_acc))
    start = (jnp.zeros((DOCS, BLOCK, KVH, HD), jnp.float32), jnp.zeros((DOCS, BLOCK, KVH, HD), jnp.float32))
    (sum_key, sum_value), (output, dquery, dkey_loc, dvalue_loc) = lax.scan(one_rollout, start, (query_all, grad_all, key_all, value_all, listed))
    attended = output.reshape(TOKENS, QH * HD)
    query_grad = dquery.reshape(TOKENS, QH * HD)
    key_grad = dkey_loc.astype(jnp.bfloat16).reshape(TOKENS, KVH * HD)
    value_grad = dvalue_loc.astype(jnp.bfloat16).reshape(TOKENS, KVH * HD)
    return (attended, query_grad, key_grad, value_grad, sum_key.reshape(DOCS * BLOCK, KVH * HD), sum_value.reshape(DOCS * BLOCK, KVH * HD))
```

```python
import functools
import math

import jax
import jax.numpy as jnp
from jax import lax
from jax.experimental import pallas as pl
from jax.experimental.pallas import tpu as pltpu
from jax.sharding import PartitionSpec as P

HD = 128
BLOCK = 128
GROUP = 8
LIST = 4
QTOK = 256
NX = 4
NY = 4
NH = 8
WIDE = GROUP * HD
ROWS = QTOK // NH
KEYS = LIST * BLOCK + QTOK
NONE = KEYS // BLOCK
MESH = pl.DeviceIdType.MESH
SCALE = 1.0 / math.sqrt(HD)
LOG2E = math.log2(math.e)
F32 = jnp.float32
BF16 = jnp.bfloat16


def roll_of(x, y, z):
    return (y * 2 + z) * NX + x


def dot(a, b, ca, cb):
    return lax.dot_general(a, b, (((ca,), (cb,)), ((), ())), preferred_element_type=F32)


def kernel(
    q_ref, g_ref, k_ref, v_ref, dk_ref, dv_ref, par_ref, slot_ref, pos_ref,
    att_ref, qg_ref, kg_ref, vg_ref, dkg_ref, dvg_ref,
    qw, gw, kw, vw, ag, sel, pool, cat, cat_t, acc, att, dq, kv_out, gs, gr, s1, r1, zs, zr,
    own_q, own_doc, head_s, head_r, z_s, z_r, one_s, one_r, two_s, two_r,
    out_s, out_r, out_l, two_bs, two_br, one_bs, one_br, zb_s, zb_r,
):
    roll = lax.axis_index("roll")
    head = lax.axis_index("head")
    x = lax.rem(roll, NX)
    zh = lax.rem(roll // NX, 2)
    y = roll // (2 * NX)
    z_dev = (roll_of(x, y, 1 - zh), head)

    place = (x, y)
    size = (NX, NY)
    docs = (dk_ref, dv_ref)

    def at(t, a, b, z):
        return roll_of(a, b, z) if t == 0 else roll_of(b, a, z)

    def first(t, d):
        a = lax.rem(place[t] + d, size[t])
        return (at(t, a, place[1 - t], zh), head)

    def second(t, d):
        b = lax.rem(place[1 - t] + d, size[1 - t])
        return (at(t, place[t], b, zh), head)

    def remote(src, dst, ss, rs, dev):
        return pltpu.make_async_remote_copy(
            src_ref=src, dst_ref=dst, send_sem=ss, recv_sem=rs, device_id=dev, device_id_type=MESH
        )

    barrier = pltpu.get_barrier_semaphore()
    partners = [z_dev]
    partners += [first(t, d) for t in range(2) for d in range(1, size[t])]
    partners += [(roll, lax.rem(head + k, NH)) for k in range(1, NH)]
    for dev in partners:
        pl.semaphore_signal(barrier, inc=1, device_id=dev, device_id_type=MESH)
    pl.semaphore_wait(barrier, len(partners))

    z_copy = []
    for t in range(2):
        c = remote(docs[t], ag.at[t, 1, place[t]], z_s.at[t], z_r.at[t], z_dev)
        c.start()
        z_copy.append(c)
    one = [[[], []], [[], []]]
    for t in range(2):
        for d in range(1, size[t]):
            c = remote(
                docs[t], ag.at[t, 0, place[t]], one_s.at[t, 0, d], one_r.at[t, 0, d], first(t, d)
            )
            c.start()
            one[t][0].append(c)
    own_docs = []
    for t in range(2):
        c = pltpu.make_async_copy(docs[t], ag.at[t, 0, place[t]], own_doc.at[t])
        c.start()
        own_docs.append(c)
    heads = []
    mine = pl.ds(pl.multiple_of(head * ROWS, ROWS), ROWS)
    for i, (src, dst, width) in enumerate(
        ((k_ref, kw, HD), (v_ref, vw, HD), (q_ref, qw, WIDE), (g_ref, gw, WIDE))
    ):
        c = pltpu.make_async_copy(
            src.at[:, pl.ds(pl.multiple_of(head * width, width), width)], dst.at[mine], own_q.at[i]
        )
        c.start()
        heads.append(c)
    sends = []
    for k in range(1, NH):
        h = lax.rem(head + k, NH)
        for i, (src, dst, width) in enumerate(
            ((k_ref, kw, HD), (v_ref, vw, HD), (q_ref, qw, WIDE), (g_ref, gw, WIDE))
        ):
            c = remote(
                src.at[:, pl.ds(pl.multiple_of(h * width, width), width)],
                dst.at[mine], head_s.at[k, i], head_r.at[k, i], (roll, h),
            )
            c.start()
            sends.append(c)

    acc[...] = jnp.zeros_like(acc)

    def slot(t, p, b, a):
        return (p * size[1 - t] + b) * size[t] + a

    def pick(t, p):
        o_z = zh if p == 0 else 1 - zh
        for d in range(size[1 - t]):
            target = second(t, d)[0]

            def step(a, _):
                pr = par_ref[target, at(t, a, place[1 - t], o_z)]
                low = ag[t, p, a, 0:BLOCK].astype(F32)
                high = ag[t, p, a, BLOCK : 2 * BLOCK].astype(F32)
                chosen = (low * (1.0 - pr) + high * pr).astype(BF16)
                if d == 0:
                    pool[t, slot(t, p, place[1 - t], a)] = chosen
                else:
                    sel[t, p, d - 1, a] = chosen
                return 0

            lax.fori_loop(0, size[t], step, 0)

    two = []
    for p in range(2):
        if p == 1:
            for t in range(2):
                z_copy[t].wait_recv()
                for d in range(1, size[t]):
                    c = remote(
                        ag.at[t, 1, place[t]], ag.at[t, 1, place[t]],
                        one_s.at[t, 1, d], one_r.at[t, 1, d], first(t, d),
                    )
                    c.start()
                    one[t][1].append(c)
        for t in range(2):
            if p == 0:
                own_docs[t].wait()
            for c in one[t][p]:
                c.wait_recv()
            pick(t, p)
            for d in range(1, size[1 - t]):
                c = remote(
                    sel.at[t, p, d - 1], pool.at[t, pl.ds(slot(t, p, place[1 - t], 0), size[t])],
                    two_s.at[t, p, d], two_r.at[t, p, d], second(t, d),
                )
                c.start()
                two.append(c)
    for c in heads:
        c.wait()
    for c in sends:
        c.wait_recv()
    for c in two:
        c.wait_recv()

    for b in range(2):
        for i in range(LIST):
            rows = pl.ds(i * BLOCK, BLOCK)
            for t in range(2):
                cat[t, b, rows] = pool[t, slot_ref[t, b * LIST + i]]
        cat[0, b, LIST * BLOCK : KEYS] = kw[...]
        cat[1, b, LIST * BLOCK : KEYS] = vw[...]
        for t in range(2):
            cat_t[t, b] = cat[t, b].T

    def compute(step, _):
        b = step // (GROUP // 2)
        c0 = pl.multiple_of(lax.rem(step, GROUP // 2) * 2 * HD, 2 * HD)
        c1 = pl.multiple_of(c0 + HD, HD)
        rows = pl.ds(pl.multiple_of(b * BLOCK, BLOCK), BLOCK)
        cols = (pl.ds(c0, HD), pl.ds(c1, HD))
        query = jnp.concatenate([qw[rows, c] for c in cols], axis=0)
        grad = jnp.concatenate([gw[rows, c] for c in cols], axis=0)
        score = dot(cat[0, b], query, 1, 1)
        local = score[LIST * BLOCK :]
        key_at = lax.broadcasted_iota(jnp.int32, local.shape, 0)
        query_at = lax.rem(lax.broadcasted_iota(jnp.int32, local.shape, 1), BLOCK) + b * BLOCK
        local = jnp.where(key_at <= query_at, local, -jnp.inf)
        score = jnp.concatenate([score[: LIST * BLOCK], local], axis=0)
        top = jnp.max(score, axis=0, keepdims=True)
        e = jnp.exp2((score - top) * (SCALE * LOG2E))
        prob = e * (1.0 / jnp.sum(e, axis=0, keepdims=True))
        weight = prob.astype(BF16)
        dprob = dot(cat[1, b], grad, 1, 1)
        delta = jnp.sum(prob * dprob, axis=0, keepdims=True)
        dscore = (prob * (dprob - delta)).astype(BF16)
        acc[1, b, 0:NONE] += dot(weight, grad, 1, 0).reshape(NONE, BLOCK, HD)
        acc[0, b, 0:NONE] += dot(dscore, query, 1, 0).reshape(NONE, BLOCK, HD)
        out_t = dot(cat_t[1, b], weight, 1, 0)
        dq_t = dot(cat_t[0, b], dscore, 1, 0) * SCALE
        for i, c in enumerate(cols):
            att[rows, c] = out_t[:, i * HD : (i + 1) * HD].T.astype(BF16)
            dq[rows, c] = dq_t[:, i * HD : (i + 1) * HD].T.astype(BF16)
        return 0

    lax.fori_loop(0, GROUP, compute, 0)

    def prepare(t, p):
        def step(n, _):
            b, a = n // size[t], lax.rem(n, size[t])
            m = p * size[0] * size[1] + n
            total = acc[t, 0, pos_ref[t, 0, m]] + acc[t, 1, pos_ref[t, 1, m]]
            if t == 0:
                total = total * SCALE
            gs[t, p, b, a] = total.astype(BF16)
            return 0

        lax.fori_loop(0, size[0] * size[1], step, 0)
        b = place[1 - t]
        gr[t, p, b] = gs[t, p, b]

    back_two = [[[], []], [[], []]]
    for p in (1, 0):
        for t in range(2):
            prepare(t, p)
            for d in range(1, size[1 - t]):
                b = lax.rem(place[1 - t] + d, size[1 - t])
                c = remote(
                    gs.at[t, p, b], gr.at[t, p, place[1 - t]],
                    two_bs.at[t, p, d], two_br.at[t, p, d], second(t, d),
                )
                c.start()
                back_two[t][p].append(c)

    for t in range(2):
        total = (acc[t, 0, LIST:NONE] + acc[t, 1, LIST:NONE]).reshape(QTOK, HD)
        if t == 0:
            total = total * SCALE
        kv_out[t] = total.astype(BF16)

    outs = []
    back = (
        (kv_out.at[0], kg_ref, HD), (kv_out.at[1], vg_ref, HD), (att, att_ref, WIDE), (dq, qg_ref, WIDE)
    )
    local_outs = []
    for i, (src, dst, width) in enumerate(back):
        there = pl.ds(pl.multiple_of(head * width, width), width)
        c = pltpu.make_async_copy(src.at[mine], dst.at[:, there], out_l.at[i])
        c.start()
        local_outs.append(c)
        for k in range(1, NH):
            h = lax.rem(head + k, NH)
            theirs = pl.ds(pl.multiple_of(h * ROWS, ROWS), ROWS)
            c = remote(
                src.at[theirs], dst.at[:, there], out_s.at[k, i], out_r.at[k, i], (roll, h)
            )
            c.start()
            outs.append(c)

    back_one = [[[], []], [[], []]]
    back_z = [None, None]
    kept = [None, None]
    for p in (1, 0):
        o_z = zh if p == 0 else 1 - zh
        for t in range(2):
            for c in back_two[t][p]:
                c.wait_recv()

            def merge(a, _):
                o = at(t, a, place[1 - t], o_z)
                low = high = jnp.zeros((BLOCK, HD), F32)
                for b in range(size[1 - t]):
                    pr = par_ref[at(t, place[t], b, zh), o]
                    m = gr[t, p, b, a].astype(F32)
                    low = low + m * (1.0 - pr)
                    high = high + m * pr
                s1[t, p, a, 0:BLOCK] = low.astype(BF16)
                s1[t, p, a, BLOCK : 2 * BLOCK] = high.astype(BF16)
                return 0

            lax.fori_loop(0, size[t], merge, 0)
            for d in range(1, size[t]):
                a = lax.rem(place[t] + d, size[t])
                c = remote(
                    s1.at[t, p, a], r1.at[t, p, place[t]],
                    one_bs.at[t, p, d], one_br.at[t, p, d], first(t, d),
                )
                c.start()
                back_one[t][p].append(c)
            r1[t, p, place[t]] = s1[t, p, place[t]]
    for p in (1, 0):
        for t in range(2):
            for c in back_one[t][p]:
                c.wait_recv()
            total = r1[t, p, 0].astype(F32)
            for a in range(1, size[t]):
                total = total + r1[t, p, a].astype(F32)
            if p == 1:
                zs[t] = total.astype(BF16)
                c = remote(zs.at[t], zr.at[t], zb_s.at[t], zb_r.at[t], z_dev)
                c.start()
                back_z[t] = c
            else:
                kept[t] = total
    for t, ref in enumerate((dkg_ref, dvg_ref)):
        back_z[t].wait_recv()
        ref[...] = kept[t] + zr[t].astype(F32)

    for c in local_outs:
        c.wait()
    for c in outs:
        c.wait_recv()
    for c in z_copy + sends + two + outs + back_z:
        c.wait_send()
    for group in (one, back_two, back_one):
        for t in range(2):
            for p in range(2):
                for c in group[t][p]:
                    c.wait_send()


def local(queries, keys, values, cotangent, doc_keys, doc_values, citations, block_lists):
    rolls = 2 * NX * NY
    roll = lax.axis_index("roll")
    zh = (roll // NX) % 2
    owner = jnp.arange(rolls, dtype=jnp.int32)
    par = jnp.sum(
        jnp.where(citations[:, None, :] // 2 == owner[None, :, None], citations[:, None, :] % 2, 0),
        axis=-1,
    ).astype(F32)
    own = lax.dynamic_slice_in_dim(citations, roll, 1, 0)[0]
    wanted = jnp.sum(
        jnp.where(
            block_lists[:, :, None] == jnp.arange(own.shape[0], dtype=jnp.int32), own[None, None, :], 0
        ),
        axis=-1,
    ) // 2
    plane = (wanted // NX) % 2 ^ zh
    wx, wy = wanted % NX, wanted // (2 * NX)
    slots = jnp.stack([(plane * NY + wy) * NX + wx, (plane * NX + wx) * NY + wy])
    pos = NONE + jnp.sum(
        jnp.where(
            slots[:, :, :, None] == owner,
            jnp.arange(LIST, dtype=jnp.int32)[None, None, :, None] - NONE,
            0,
        ),
        axis=2,
    )
    slots = slots.reshape(2, 2 * LIST)
    n = max(NX, NY)
    any_spec = pl.BlockSpec(memory_space=pltpu.HBM)
    vmem = pl.BlockSpec(memory_space=pltpu.VMEM)
    smem = pl.BlockSpec(memory_space=pltpu.SMEM)
    dma = pltpu.SemaphoreType.DMA
    blk = (BLOCK, HD)
    sd = jax.ShapeDtypeStruct
    return pl.pallas_call(
        kernel,
        out_shape=(
            sd(queries.shape, BF16), sd(queries.shape, BF16), sd(keys.shape, BF16), sd(keys.shape, BF16),
            sd(doc_keys.shape, F32), sd(doc_keys.shape, F32),
        ),
        in_specs=[any_spec] * 6 + [smem] * 3,
        out_specs=(any_spec,) * 4 + (vmem,) * 2,
        scratch_shapes=[
            pltpu.VMEM((QTOK, WIDE), BF16),
            pltpu.VMEM((QTOK, WIDE), BF16),
            pltpu.VMEM((QTOK, HD), BF16),
            pltpu.VMEM((QTOK, HD), BF16),
            pltpu.VMEM((2, 2, n, 2 * BLOCK, HD), BF16),
            pltpu.VMEM((2, 2, n - 1, n) + blk, BF16),
            pltpu.VMEM((2, 2 * n * n) + blk, BF16),
            pltpu.VMEM((2, 2, KEYS, HD), BF16),
            pltpu.VMEM((2, 2, HD, KEYS), BF16),
            pltpu.VMEM((2, 2, NONE + 1) + blk, F32),
            pltpu.VMEM((QTOK, WIDE), BF16),
            pltpu.VMEM((QTOK, WIDE), BF16),
            pltpu.VMEM((2, QTOK, HD), BF16),
            pltpu.VMEM((2, 2, n, n) + blk, BF16),
            pltpu.VMEM((2, 2, n, n) + blk, BF16),
            pltpu.VMEM((2, 2, n, 2 * BLOCK, HD), BF16),
            pltpu.VMEM((2, 2, n, 2 * BLOCK, HD), BF16),
            pltpu.VMEM((2, 2 * BLOCK, HD), BF16),
            pltpu.VMEM((2, 2 * BLOCK, HD), BF16),
            dma((4,)), dma((2,)), dma((NH, 4)), dma((NH, 4)), dma((2,)), dma((2,)),
            dma((2, 2, n)), dma((2, 2, n)), dma((2, 2, n)), dma((2, 2, n)),
            dma((NH, 4)), dma((NH, 4)), dma((4,)),
            dma((2, 2, n)), dma((2, 2, n)), dma((2, 2, n)), dma((2, 2, n)), dma((2,)), dma((2,)),
        ],
        compiler_params=pltpu.CompilerParams(
            collective_id=0, has_side_effects=True, vmem_limit_bytes=48 * 2**20
        ),
        name="attention",
    )(queries, cotangent, keys, values, doc_keys, doc_values, par, slots, pos)


def solution(mesh):
    return jax.shard_map(
        local,
        mesh=mesh,
        in_specs=(
            P(("roll", "head"), None),
            P(("roll", "head"), None),
            P(("roll", "head"), None),
            P(("roll", "head"), None),
            P("roll", "head"),
            P("roll", "head"),
            P(),
            P("roll", None),
        ),
        out_specs=(
            P(("roll", "head"), None),
            P(("roll", "head"), None),
            P(("roll", "head"), None),
            P(("roll", "head"), None),
            P("roll", "head"),
            P("roll", "head"),
        ),
        check_vma=False,
    )
```

```python
import functools
import math

import jax
import jax.numpy as jnp
from jax import lax
from jax.experimental import pallas as pl
from jax.experimental.pallas import tpu as pltpu
from jax.sharding import PartitionSpec as P

HD = 128
BLOCK = 128
GROUP = 8
LIST = 4
QTOK = 256
NX = 4
NY = 4
NH = 8
WIDE = GROUP * HD
ROWS = QTOK // NH
KEYS = LIST * BLOCK + QTOK
NONE = KEYS // BLOCK
PAIR = 2 * HD
STEPS = GROUP // 2
MESH = pl.DeviceIdType.MESH
SCALE = 1.0 / math.sqrt(HD)
LOG2E = math.log2(math.e)
F32 = jnp.float32
BF16 = jnp.bfloat16


def roll_of(x, y, z):
    return (y * 2 + z) * NX + x


def dot(a, b, ca, cb):
    return lax.dot_general(a, b, (((ca,), (cb,)), ((), ())), preferred_element_type=F32)


def kernel(
    q_ref, g_ref, k_ref, v_ref, dk_ref, dv_ref, cite_v_ref, cite_ref, list_ref,
    att_ref, qg_ref, kg_ref, vg_ref, dkg_ref, dvg_ref,
    qw, gw, kw, vw, ag, sel, pool, cat, cat_t, acc, att, dq, kv_out, gs, gr, s1, r1, zs, zr,
    par_v, par_ref, par_sem, own_q, own_doc, kv_s, kv_r, head_s, head_r, z_s, z_r, one_s, one_r, two_s, two_r,
    kvo_s, kvo_r, out_s, out_r, out_l, two_bs, two_br, one_bs, one_br, zb_s, zb_r,
):
    roll = lax.axis_index("roll")
    head = lax.axis_index("head")
    x = lax.rem(roll, NX)
    zh = lax.rem(roll // NX, 2)
    y = roll // (2 * NX)
    z_dev = (roll_of(x, y, 1 - zh), head)

    place = (x, y)
    size = (NX, NY)
    docs = (dk_ref, dv_ref)

    def at(t, a, b, z):
        return roll_of(a, b, z) if t == 0 else roll_of(b, a, z)

    def first(t, d):
        a = lax.rem(place[t] + d, size[t])
        return (at(t, a, place[1 - t], zh), head)

    def second(t, d):
        b = lax.rem(place[1 - t] + d, size[1 - t])
        return (at(t, place[t], b, zh), head)

    def remote(src, dst, ss, rs, dev):
        return pltpu.make_async_remote_copy(
            src_ref=src, dst_ref=dst, send_sem=ss, recv_sem=rs, device_id=dev, device_id_type=MESH
        )

    acc[...] = jnp.zeros_like(acc)

    cites = cite_v_ref[...]
    rolls = 2 * NX * NY
    owner_at = lax.broadcasted_iota(jnp.int32, (rolls, HD), 1)
    odd = jnp.zeros((rolls, HD), jnp.int32)
    for c in range(cites.shape[1]):
        cite = cites[:, c : c + 1]
        odd = odd + jnp.where((cite >> 1) == owner_at, cite & 1, 0)

    barrier = pltpu.get_barrier_semaphore()
    partners = [z_dev]
    partners += [first(t, d) for t in range(2) for d in range(1, size[t])]
    partners += [(roll, lax.rem(head + k, NH)) for k in range(1, NH)]
    for dev in partners:
        pl.semaphore_signal(barrier, inc=1, device_id=dev, device_id_type=MESH)
    pl.semaphore_wait(barrier, len(partners))

    par_v[...] = odd.astype(F32)
    par_copy = pltpu.make_async_copy(par_v, par_ref, par_sem.at[0])

    z_copy = []
    for t in range(2):
        c = remote(docs[t], ag.at[t, 1, place[t]], z_s.at[t], z_r.at[t], z_dev)
        c.start()
        z_copy.append(c)
    one = [[[], []], [[], []]]
    for t in range(2):
        for d in range(1, size[t]):
            c = remote(
                docs[t], ag.at[t, 0, place[t]], one_s.at[t, 0, d], one_r.at[t, 0, d], first(t, d)
            )
            c.start()
            one[t][0].append(c)
    own_docs = []
    for t in range(2):
        c = pltpu.make_async_copy(docs[t], ag.at[t, 0, place[t]], own_doc.at[t])
        c.start()
        own_docs.append(c)
    par_copy.start()
    heads = []
    mine = pl.ds(pl.multiple_of(head * ROWS, ROWS), ROWS)
    moved = ((k_ref, kw, HD), (v_ref, vw, HD), (q_ref, qw, WIDE), (g_ref, gw, WIDE))
    for i, (src, dst, width) in enumerate(moved):
        c = pltpu.make_async_copy(
            src.at[:, pl.ds(pl.multiple_of(head * width, width), width)], dst.at[mine], own_q.at[i]
        )
        c.start()
        heads.append(c)

    def kv_copy(k, i):
        h = lax.rem(head + k, NH)
        src, dst, width = moved[i]
        return remote(
            src.at[:, pl.ds(pl.multiple_of(h * width, width), width)],
            dst.at[mine], kv_s.at[k, i], kv_r.at[k, i], (roll, h),
        )

    def chunk_copy(k, i, j):
        h = lax.rem(head + k, NH)
        src, dst, width = moved[2 + i]
        return remote(
            src.at[:, pl.ds(pl.multiple_of(h * width + j * PAIR, PAIR), PAIR)],
            dst.at[mine, pl.ds(pl.multiple_of(j * PAIR, PAIR), PAIR)],
            head_s.at[k, i, j], head_r.at[k, i, j], (roll, h),
        )

    for k in range(1, NH):
        for i in range(2):
            kv_copy(k, i).start()

    def send_chunks(j, _):
        for k in range(1, NH):
            for i in range(2):
                chunk_copy(k, i, j).start()
        return 0

    lax.fori_loop(0, STEPS, send_chunks, 0)

    par_copy.wait()

    def slot(t, p, b, a):
        return (p * size[1 - t] + b) * size[t] + a

    def pick(t, p):
        o_z = zh if p == 0 else 1 - zh
        for d in range(size[1 - t]):
            target = second(t, d)[0]

            def step(a, _):
                pr = par_ref[target, at(t, a, place[1 - t], o_z)]
                low = ag[t, p, a, 0:BLOCK].astype(F32)
                high = ag[t, p, a, BLOCK : 2 * BLOCK].astype(F32)
                chosen = (low * (1.0 - pr) + high * pr).astype(BF16)
                if d == 0:
                    pool[t, slot(t, p, place[1 - t], a)] = chosen
                else:
                    sel[t, p, d - 1, a] = chosen
                return 0

            lax.fori_loop(0, size[t], step, 0)

    two = []
    for p in range(2):
        if p == 1:
            for t in range(2):
                z_copy[t].wait_recv()
                for d in range(1, size[t]):
                    c = remote(
                        ag.at[t, 1, place[t]], ag.at[t, 1, place[t]],
                        one_s.at[t, 1, d], one_r.at[t, 1, d], first(t, d),
                    )
                    c.start()
                    one[t][1].append(c)
        for t in range(2):
            if p == 0:
                own_docs[t].wait()
            for c in one[t][p]:
                c.wait_recv()
            pick(t, p)
            for d in range(1, size[1 - t]):
                c = remote(
                    sel.at[t, p, d - 1], pool.at[t, pl.ds(slot(t, p, place[1 - t], 0), size[t])],
                    two_s.at[t, p, d], two_r.at[t, p, d], second(t, d),
                )
                c.start()
                two.append(c)
    for c in heads:
        c.wait()
    for k in range(1, NH):
        for i in range(2):
            kv_copy(k, i).wait_recv()
    for c in two:
        c.wait_recv()

    owners = []
    for b in range(2):
        for i in range(LIST):
            o = cite_ref[roll, list_ref[b, i]] >> 1
            owners.append(o)
            ox, oz, oy = o & (NX - 1), (o // NX) & 1, o // (2 * NX)
            slots = [((oz ^ zh) * NY + oy) * NX + ox, ((oz ^ zh) * NX + ox) * NY + oy]
            rows = pl.ds(i * BLOCK, BLOCK)
            for t in range(2):
                cat[t, b, rows] = pool[t, slots[t]]
        cat[0, b, LIST * BLOCK : KEYS] = kw[...]
        cat[1, b, LIST * BLOCK : KEYS] = vw[...]
        for t in range(2):
            cat_t[t, b] = cat[t, b].T

    def compute(b, j):
        c0 = pl.multiple_of(j * PAIR, PAIR)
        c1 = pl.multiple_of(c0 + HD, HD)
        rows = pl.ds(pl.multiple_of(b * BLOCK, BLOCK), BLOCK)
        cols = (pl.ds(c0, HD), pl.ds(c1, HD))
        query = jnp.concatenate([qw[rows, c] for c in cols], axis=0)
        grad = jnp.concatenate([gw[rows, c] for c in cols], axis=0)
        score = dot(cat[0, b], query, 1, 1)
        local = score[LIST * BLOCK :]
        key_at = lax.broadcasted_iota(jnp.int32, local.shape, 0)
        query_at = lax.rem(lax.broadcasted_iota(jnp.int32, local.shape, 1), BLOCK) + b * BLOCK
        local = jnp.where(key_at <= query_at, local, -jnp.inf)
        score = jnp.concatenate([score[: LIST * BLOCK], local], axis=0)
        top = jnp.max(score, axis=0, keepdims=True)
        e = jnp.exp2((score - top) * (SCALE * LOG2E))
        prob = e * (1.0 / jnp.sum(e, axis=0, keepdims=True))
        weight = prob.astype(BF16)
        dprob = dot(cat[1, b], grad, 1, 1)
        delta = jnp.sum(prob * dprob, axis=0, keepdims=True)
        dscore = (prob * (dprob - delta)).astype(BF16)
        acc[1, b, 0:NONE] += dot(weight, grad, 1, 0).reshape(NONE, BLOCK, HD)
        acc[0, b, 0:NONE] += dot(dscore, query, 1, 0).reshape(NONE, BLOCK, HD)
        out_t = dot(cat_t[1, b], weight, 1, 0)
        dq_t = dot(cat_t[0, b], dscore, 1, 0) * SCALE
        for i, c in enumerate(cols):
            att[rows, c] = out_t[:, i * HD : (i + 1) * HD].T.astype(BF16)
            dq[rows, c] = dq_t[:, i * HD : (i + 1) * HD].T.astype(BF16)

    back = ((att, att_ref, WIDE), (dq, qg_ref, WIDE), (kv_out.at[0], kg_ref, HD), (kv_out.at[1], vg_ref, HD))

    def own_out(i):
        src, dst, width = back[i]
        there = pl.ds(pl.multiple_of(head * width, width), width)
        return pltpu.make_async_copy(src.at[mine], dst.at[:, there], out_l.at[i])

    def kv_back(k, i):
        h = lax.rem(head + k, NH)
        src, dst, width = back[2 + i]
        theirs = pl.ds(pl.multiple_of(h * ROWS, ROWS), ROWS)
        there = pl.ds(pl.multiple_of(head * width, width), width)
        return remote(src.at[theirs], dst.at[:, there], kvo_s.at[k, i], kvo_r.at[k, i], (roll, h))

    def chunk_back(k, i, j):
        h = lax.rem(head + k, NH)
        src, dst, width = back[i]
        theirs = pl.ds(pl.multiple_of(h * ROWS, ROWS), ROWS)
        return remote(
            src.at[theirs, pl.ds(pl.multiple_of(j * PAIR, PAIR), PAIR)],
            dst.at[:, pl.ds(pl.multiple_of(head * width + j * PAIR, PAIR), PAIR)],
            out_s.at[k, i, j], out_r.at[k, i, j], (roll, h),
        )

    def per_chunk(j, _):
        for k in range(1, NH):
            for i in range(2):
                chunk_copy(k, i, j).wait_recv()

        def per_block(b, _):
            compute(b, j)
            return 0

        lax.fori_loop(0, 2, per_block, 0)
        for k in range(1, NH):
            for i in range(2):
                chunk_back(k, i, j).start()
        return 0

    lax.fori_loop(0, STEPS, per_chunk, 0)

    def prepare(t, p):
        def step(n, _):
            b, a = n // size[t], lax.rem(n, size[t])
            o = at(t, a, b, zh if p == 0 else 1 - zh)
            pos = []
            for blk in range(2):
                at_list = jnp.int32(NONE)
                for i in range(LIST):
                    same = (owners[blk * LIST + i] == o).astype(jnp.int32)
                    at_list = at_list + same * (i - at_list)
                pos.append(at_list)
            total = acc[t, 0, pos[0]] + acc[t, 1, pos[1]]
            if t == 0:
                total = total * SCALE
            gs[t, p, b, a] = total.astype(BF16)
            return 0

        lax.fori_loop(0, size[0] * size[1], step, 0)
        b = place[1 - t]
        gr[t, p, b] = gs[t, p, b]

    back_two = [[[], []], [[], []]]
    for p in (1, 0):
        for t in range(2):
            prepare(t, p)
            for d in range(1, size[1 - t]):
                b = lax.rem(place[1 - t] + d, size[1 - t])
                c = remote(
                    gs.at[t, p, b], gr.at[t, p, place[1 - t]],
                    two_bs.at[t, p, d], two_br.at[t, p, d], second(t, d),
                )
                c.start()
                back_two[t][p].append(c)

    for t in range(2):
        total = (acc[t, 0, LIST:NONE] + acc[t, 1, LIST:NONE]).reshape(QTOK, HD)
        if t == 0:
            total = total * SCALE
        kv_out[t] = total.astype(BF16)

    for i in range(4):
        own_out(i).start()
    for k in range(1, NH):
        for i in range(2):
            kv_back(k, i).start()

    back_one = [[[], []], [[], []]]
    back_z = [None, None]
    kept = [None, None]
    for p in (1, 0):
        o_z = zh if p == 0 else 1 - zh
        for t in range(2):
            for c in back_two[t][p]:
                c.wait_recv()

            def merge(a, _):
                o = at(t, a, place[1 - t], o_z)
                low = high = jnp.zeros((BLOCK, HD), F32)
                for b in range(size[1 - t]):
                    pr = par_ref[at(t, place[t], b, zh), o]
                    m = gr[t, p, b, a].astype(F32)
                    low = low + m * (1.0 - pr)
                    high = high + m * pr
                s1[t, p, a, 0:BLOCK] = low.astype(BF16)
                s1[t, p, a, BLOCK : 2 * BLOCK] = high.astype(BF16)
                return 0

            lax.fori_loop(0, size[t], merge, 0)
            for d in range(1, size[t]):
                a = lax.rem(place[t] + d, size[t])
                c = remote(
                    s1.at[t, p, a], r1.at[t, p, place[t]],
                    one_bs.at[t, p, d], one_br.at[t, p, d], first(t, d),
                )
                c.start()
                back_one[t][p].append(c)
            r1[t, p, place[t]] = s1[t, p, place[t]]
    for p in (1, 0):
        for t in range(2):
            for c in back_one[t][p]:
                c.wait_recv()
            total = r1[t, p, 0].astype(F32)
            for a in range(1, size[t]):
                total = total + r1[t, p, a].astype(F32)
            if p == 1:
                zs[t] = total.astype(BF16)
                c = remote(zs.at[t], zr.at[t], zb_s.at[t], zb_r.at[t], z_dev)
                c.start()
                back_z[t] = c
            else:
                kept[t] = total
    for t, ref in enumerate((dkg_ref, dvg_ref)):
        back_z[t].wait_recv()
        ref[...] = kept[t] + zr[t].astype(F32)

    for i in range(4):
        own_out(i).wait()
    for k in range(1, NH):
        for i in range(2):
            kv_copy(k, i).wait_send()
            kv_back(k, i).wait()

    def drain(j, _):
        for k in range(1, NH):
            for i in range(2):
                chunk_copy(k, i, j).wait_send()
                chunk_back(k, i, j).wait()
        return 0

    lax.fori_loop(0, STEPS, drain, 0)
    for c in z_copy + two + back_z:
        c.wait_send()
    for group in (one, back_two, back_one):
        for t in range(2):
            for p in range(2):
                for c in group[t][p]:
                    c.wait_send()


def copy_out(*refs):
    n = len(refs) // 2
    copies = [pltpu.make_async_copy(refs[i], refs[n + i], refs[-1].at[i]) for i in range(n)]
    for c in copies:
        c.start()
    for c in copies:
        c.wait()


def local(queries, keys, values, cotangent, doc_keys, doc_values, citations, block_lists):
    n = max(NX, NY)
    any_spec = pl.BlockSpec(memory_space=pltpu.HBM)
    vmem = pl.BlockSpec(memory_space=pltpu.VMEM)
    smem = pl.BlockSpec(memory_space=pltpu.SMEM)
    dma = pltpu.SemaphoreType.DMA
    blk = (BLOCK, HD)
    sd = jax.ShapeDtypeStruct
    results = pl.pallas_call(
        kernel,
        out_shape=(
            sd(queries.shape, BF16), sd(queries.shape, BF16), sd(keys.shape, BF16), sd(keys.shape, BF16),
            sd(doc_keys.shape, F32), sd(doc_keys.shape, F32),
        ),
        in_specs=[any_spec] * 6 + [vmem, smem, smem],
        out_specs=(any_spec,) * 4 + (vmem,) * 2,
        scratch_shapes=[
            pltpu.VMEM((QTOK, WIDE), BF16),
            pltpu.VMEM((QTOK, WIDE), BF16),
            pltpu.VMEM((QTOK, HD), BF16),
            pltpu.VMEM((QTOK, HD), BF16),
            pltpu.VMEM((2, 2, n, 2 * BLOCK, HD), BF16),
            pltpu.VMEM((2, 2, n - 1, n) + blk, BF16),
            pltpu.VMEM((2, 2 * n * n) + blk, BF16),
            pltpu.VMEM((2, 2, KEYS, HD), BF16),
            pltpu.VMEM((2, 2, HD, KEYS), BF16),
            pltpu.VMEM((2, 2, NONE + 1) + blk, F32),
            pltpu.VMEM((QTOK, WIDE), BF16),
            pltpu.VMEM((QTOK, WIDE), BF16),
            pltpu.VMEM((2, QTOK, HD), BF16),
            pltpu.VMEM((2, 2, n, n) + blk, BF16),
            pltpu.VMEM((2, 2, n, n) + blk, BF16),
            pltpu.VMEM((2, 2, n, 2 * BLOCK, HD), BF16),
            pltpu.VMEM((2, 2, n, 2 * BLOCK, HD), BF16),
            pltpu.VMEM((2, 2 * BLOCK, HD), BF16),
            pltpu.VMEM((2, 2 * BLOCK, HD), BF16),
            pltpu.VMEM((2 * NX * NY, HD), F32),
            pltpu.SMEM((2 * NX * NY, HD), F32),
            dma((1,)),
            dma((4,)), dma((2,)), dma((NH, 2)), dma((NH, 2)), dma((NH, 2, STEPS)), dma((NH, 2, STEPS)),
            dma((2,)), dma((2,)),
            dma((2, 2, n)), dma((2, 2, n)), dma((2, 2, n)), dma((2, 2, n)),
            dma((NH, 2)), dma((NH, 2)), dma((NH, 2, STEPS)), dma((NH, 2, STEPS)), dma((4,)),
            dma((2, 2, n)), dma((2, 2, n)), dma((2, 2, n)), dma((2, 2, n)), dma((2,)), dma((2,)),
        ],
        compiler_params=pltpu.CompilerParams(
            collective_id=0, has_side_effects=True, vmem_limit_bytes=60 * 2**20
        ),
        name="attention",
    )(queries, cotangent, keys, values, doc_keys, doc_values, citations, citations, block_lists)
    return pl.pallas_call(
        copy_out,
        out_shape=tuple(sd(r.shape, r.dtype) for r in results),
        in_specs=[any_spec] * 6,
        out_specs=(any_spec,) * 6,
        scratch_shapes=[dma((6,))],
        compiler_params=pltpu.CompilerParams(vmem_limit_bytes=60 * 2**20),
        name="copy_out",
    )(*results)


def solution(mesh):
    return jax.shard_map(
        local,
        mesh=mesh,
        in_specs=(
            P(("roll", "head"), None),
            P(("roll", "head"), None),
            P(("roll", "head"), None),
            P(("roll", "head"), None),
            P("roll", "head"),
            P("roll", "head"),
            P(),
            P("roll", None),
        ),
        out_specs=(
            P(("roll", "head"), None),
            P(("roll", "head"), None),
            P(("roll", "head"), None),
            P(("roll", "head"), None),
            P("roll", "head"),
            P("roll", "head"),
        ),
        check_vma=False,
    )
```

```python
import functools
import math

import jax
import jax.numpy as jnp
from jax import lax
from jax.experimental import pallas as pl
from jax.experimental.pallas import tpu as pltpu
from jax.sharding import PartitionSpec as P

HD = 128
BLOCK = 128
GROUP = 8
LIST = 4
QTOK = 256
NX = 4
NY = 4
NH = 8
WIDE = GROUP * HD
ROWS = QTOK // NH
KEYS = LIST * BLOCK + QTOK
NONE = KEYS // BLOCK
PAIR = 2 * HD
STEPS = GROUP // 2
EARLY = 1
MIDDLE = 4
MESH = pl.DeviceIdType.MESH
SCALE = 1.0 / math.sqrt(HD)
LOG2E = math.log2(math.e)
F32 = jnp.float32
BF16 = jnp.bfloat16


def roll_of(x, y, z):
    return (y * 2 + z) * NX + x


def dot(a, b, ca, cb):
    return lax.dot_general(a, b, (((ca,), (cb,)), ((), ())), preferred_element_type=F32)


def kernel(
    q_ref, g_ref, k_ref, v_ref, dk_ref, dv_ref, cite_v_ref, cite_ref, list_ref,
    att_ref, qg_ref, kg_ref, vg_ref, dkg_ref, dvg_ref,
    qw, gw, kw, vw, ag, sel, pool, cat, cat_t, acc, att, dq, kv_out, gs, gr, s1, r1, zs, zr,
    par_v, par_ref, par_sem, own_q, own_doc, kv_s, kv_r, head_s, head_r, z_s, z_r, one_s, one_r, two_s, two_r,
    kvo_s, kvo_r, out_s, out_r, out_l, two_bs, two_br, one_bs, one_br, zb_s, zb_r,
):
    roll = lax.axis_index("roll")
    head = lax.axis_index("head")
    x = lax.rem(roll, NX)
    zh = lax.rem(roll // NX, 2)
    y = roll // (2 * NX)
    z_dev = (roll_of(x, y, 1 - zh), head)

    place = (x, y)
    size = (NX, NY)
    docs = (dk_ref, dv_ref)

    def at(t, a, b, z):
        return roll_of(a, b, z) if t == 0 else roll_of(b, a, z)

    def first(t, d):
        a = lax.rem(place[t] + d, size[t])
        return (at(t, a, place[1 - t], zh), head)

    def second(t, d):
        b = lax.rem(place[1 - t] + d, size[1 - t])
        return (at(t, place[t], b, zh), head)

    def remote(src, dst, ss, rs, dev):
        return pltpu.make_async_remote_copy(
            src_ref=src, dst_ref=dst, send_sem=ss, recv_sem=rs, device_id=dev, device_id_type=MESH
        )

    barrier = pltpu.get_barrier_semaphore()
    partners = [z_dev]
    partners += [first(t, d) for t in range(2) for d in range(1, size[t])]
    partners += [(roll, lax.rem(head + k, NH)) for k in range(1, NH)]
    for dev in partners:
        pl.semaphore_signal(barrier, inc=1, device_id=dev, device_id_type=MESH)

    acc[...] = jnp.zeros_like(acc)

    cites = cite_v_ref[...]
    rolls = 2 * NX * NY
    owner_at = lax.broadcasted_iota(jnp.int32, (rolls, rolls), 0)
    odd = jnp.zeros((rolls, rolls), jnp.int32)
    for c in range(cites.shape[0]):
        cite = cites[c : c + 1]
        odd = odd + jnp.where((cite >> 1) == owner_at, cite & 1, 0)

    pl.semaphore_wait(barrier, len(partners))

    par_v[:, 0:rolls] = odd.astype(F32)
    par_copy = pltpu.make_async_copy(par_v, par_ref, par_sem.at[0])

    z_copy = []
    for t in range(2):
        c = remote(docs[t], ag.at[t, 1, place[t]], z_s.at[t], z_r.at[t], z_dev)
        c.start()
        z_copy.append(c)
    one = [[[], []], [[], []]]
    for t in range(2):
        for d in range(1, size[t]):
            c = remote(
                docs[t], ag.at[t, 0, place[t]], one_s.at[t, 0, d], one_r.at[t, 0, d], first(t, d)
            )
            c.start()
            one[t][0].append(c)
    own_docs = []
    for t in range(2):
        c = pltpu.make_async_copy(docs[t], ag.at[t, 0, place[t]], own_doc.at[t])
        c.start()
        own_docs.append(c)
    par_copy.start()
    heads = []
    mine = pl.ds(pl.multiple_of(head * ROWS, ROWS), ROWS)
    moved = ((k_ref, kw, HD), (v_ref, vw, HD), (q_ref, qw, WIDE), (g_ref, gw, WIDE))
    for i, (src, dst, width) in enumerate(moved):
        c = pltpu.make_async_copy(
            src.at[:, pl.ds(pl.multiple_of(head * width, width), width)], dst.at[mine], own_q.at[i]
        )
        c.start()
        heads.append(c)

    def kv_copy(k, i):
        h = lax.rem(head + k, NH)
        src, dst, width = moved[i]
        return remote(
            src.at[:, pl.ds(pl.multiple_of(h * width, width), width)],
            dst.at[mine], kv_s.at[k, i], kv_r.at[k, i], (roll, h),
        )

    def chunk_copy(k, i, j):
        h = lax.rem(head + k, NH)
        src, dst, width = moved[2 + i]
        return remote(
            src.at[:, pl.ds(pl.multiple_of(h * width + j * PAIR, PAIR), PAIR)],
            dst.at[mine, pl.ds(pl.multiple_of(j * PAIR, PAIR), PAIR)],
            head_s.at[k, i, j], head_r.at[k, i, j], (roll, h),
        )

    for k in range(1, NH):
        for i in range(2):
            kv_copy(k, i).start()

    def send_chunks(j, _):
        for k in range(1, NH):
            for i in range(2):
                chunk_copy(k, i, j).start()
        return 0

    lax.fori_loop(0, STEPS, send_chunks, 0)

    par_copy.wait()

    def slot(t, p, b, a):
        return (p * size[1 - t] + b) * size[t] + a

    def pick(t, p):
        o_z = zh if p == 0 else 1 - zh
        for d in range(size[1 - t]):
            target = second(t, d)[0]

            def step(a, _):
                pr = par_ref[at(t, a, place[1 - t], o_z), target]
                low = ag[t, p, a, 0:BLOCK].astype(F32)
                high = ag[t, p, a, BLOCK : 2 * BLOCK].astype(F32)
                chosen = (low * (1.0 - pr) + high * pr).astype(BF16)
                if d == 0:
                    pool[t, slot(t, p, place[1 - t], a)] = chosen
                else:
                    sel[t, p, d - 1, a] = chosen
                return 0

            lax.fori_loop(0, size[t], step, 0)

    two = []
    for p in range(2):
        if p == 1:
            for t in range(2):
                z_copy[t].wait_recv()
                for d in range(1, size[t]):
                    c = remote(
                        ag.at[t, 1, place[t]], ag.at[t, 1, place[t]],
                        one_s.at[t, 1, d], one_r.at[t, 1, d], first(t, d),
                    )
                    c.start()
                    one[t][1].append(c)
        for t in range(2):
            if p == 0:
                own_docs[t].wait()
            for c in one[t][p]:
                c.wait_recv()
            pick(t, p)
            for d in range(1, size[1 - t]):
                c = remote(
                    sel.at[t, p, d - 1], pool.at[t, pl.ds(slot(t, p, place[1 - t], 0), size[t])],
                    two_s.at[t, p, d], two_r.at[t, p, d], second(t, d),
                )
                c.start()
                two.append(c)
    for c in heads:
        c.wait()
    for k in range(1, NH):
        for i in range(2):
            kv_copy(k, i).wait_recv()
    for c in two:
        c.wait_recv()

    owners = []
    for b in range(2):
        for i in range(LIST):
            o = cite_ref[list_ref[b, i], roll] >> 1
            owners.append(o)
            ox, oz, oy = o & (NX - 1), (o // NX) & 1, o // (2 * NX)
            slots = [((oz ^ zh) * NY + oy) * NX + ox, ((oz ^ zh) * NX + ox) * NY + oy]
            rows = pl.ds(i * BLOCK, BLOCK)
            for t in range(2):
                cat[t, b, rows] = pool[t, slots[t]]
        cat[0, b, LIST * BLOCK : KEYS] = kw[...]
        cat[1, b, LIST * BLOCK : KEYS] = vw[...]
        for t in range(2):
            cat_t[t, b] = cat[t, b].T

    def compute(b, j):
        c0 = pl.multiple_of(j * PAIR, PAIR)
        c1 = pl.multiple_of(c0 + HD, HD)
        rows = pl.ds(pl.multiple_of(b * BLOCK, BLOCK), BLOCK)
        cols = (pl.ds(c0, HD), pl.ds(c1, HD))
        query = jnp.concatenate([qw[rows, c] for c in cols], axis=0)
        grad = jnp.concatenate([gw[rows, c] for c in cols], axis=0)
        score = dot(cat[0, b], query, 1, 1)
        local = score[LIST * BLOCK :]
        key_at = lax.broadcasted_iota(jnp.int32, local.shape, 0)
        query_at = lax.rem(lax.broadcasted_iota(jnp.int32, local.shape, 1), BLOCK) + b * BLOCK
        local = jnp.where(key_at <= query_at, local, -jnp.inf)
        score = jnp.concatenate([score[: LIST * BLOCK], local], axis=0)
        top = jnp.max(score, axis=0, keepdims=True)
        e = jnp.exp2((score - top) * (SCALE * LOG2E))
        prob = e * (1.0 / jnp.sum(e, axis=0, keepdims=True))
        weight = prob.astype(BF16)
        dprob = dot(cat[1, b], grad, 1, 1)
        delta = jnp.sum(prob * dprob, axis=0, keepdims=True)
        dscore = (prob * (dprob - delta)).astype(BF16)
        acc[1, b, 0:NONE] += dot(weight, grad, 1, 0).reshape(NONE, BLOCK, HD)
        acc[0, b, 0:NONE] += dot(dscore, query, 1, 0).reshape(NONE, BLOCK, HD)
        out_t = dot(cat_t[1, b], weight, 1, 0)
        dq_t = dot(cat_t[0, b], dscore, 1, 0) * SCALE
        for i, c in enumerate(cols):
            att[rows, c] = out_t[:, i * HD : (i + 1) * HD].T.astype(BF16)
            dq[rows, c] = dq_t[:, i * HD : (i + 1) * HD].T.astype(BF16)

    back = ((att, att_ref, WIDE), (dq, qg_ref, WIDE), (kv_out.at[0], kg_ref, HD), (kv_out.at[1], vg_ref, HD))

    def own_out(i):
        src, dst, width = back[i]
        there = pl.ds(pl.multiple_of(head * width, width), width)
        return pltpu.make_async_copy(src.at[mine], dst.at[:, there], out_l.at[i])

    def kv_back(k, i):
        h = lax.rem(head + k, NH)
        src, dst, width = back[2 + i]
        theirs = pl.ds(pl.multiple_of(h * ROWS, ROWS), ROWS)
        there = pl.ds(pl.multiple_of(head * width, width), width)
        return remote(src.at[theirs], dst.at[:, there], kvo_s.at[k, i], kvo_r.at[k, i], (roll, h))

    def chunk_back(k, i, j):
        h = lax.rem(head + k, NH)
        src, dst, width = back[i]
        theirs = pl.ds(pl.multiple_of(h * ROWS, ROWS), ROWS)
        return remote(
            src.at[theirs, pl.ds(pl.multiple_of(j * PAIR, PAIR), PAIR)],
            dst.at[:, pl.ds(pl.multiple_of(head * width + j * PAIR, PAIR), PAIR)],
            out_s.at[k, i, j], out_r.at[k, i, j], (roll, h),
        )

    def send_back(j, _):
        for k in range(1, NH):
            for i in range(2):
                chunk_back(k, i, j).start()
        return 0

    def per_chunk(j, _):
        for k in range(1, NH):
            for i in range(2):
                chunk_copy(k, i, j).wait_recv()

        def per_block(b, _):
            compute(b, j)
            return 0

        lax.fori_loop(0, 2, per_block, 0)
        @pl.when(j < EARLY)
        def _():
            send_back(j, 0)

        return 0

    lax.fori_loop(0, STEPS, per_chunk, 0)

    def prepare(t, p, b):
        def step(a, _):
            o = at(t, a, b, zh if p == 0 else 1 - zh)
            pos = []
            for blk in range(2):
                at_list = jnp.int32(NONE)
                for i in range(LIST):
                    same = (owners[blk * LIST + i] == o).astype(jnp.int32)
                    at_list = at_list + same * (i - at_list)
                pos.append(at_list)
            total = acc[t, 0, pos[0]] + acc[t, 1, pos[1]]
            if t == 0:
                total = total * SCALE
            gs[t, p, b, a] = total.astype(BF16)
            return 0

        lax.fori_loop(0, size[t], step, 0)

    back_two = [[[], []], [[], []]]
    for p in (1, 0):
        for d in range(1, NX):
            for t in range(2):
                b = lax.rem(place[1 - t] + d, size[1 - t])
                prepare(t, p, b)
                c = remote(
                    gs.at[t, p, b], gr.at[t, p, place[1 - t]],
                    two_bs.at[t, p, d], two_br.at[t, p, d], second(t, d),
                )
                c.start()
                back_two[t][p].append(c)
    lax.fori_loop(EARLY, MIDDLE, send_back, 0)
    for p in (1, 0):
        for t in range(2):
            b = place[1 - t]
            prepare(t, p, b)
            gr[t, p, b] = gs[t, p, b]

    for t in range(2):
        total = (acc[t, 0, LIST:NONE] + acc[t, 1, LIST:NONE]).reshape(QTOK, HD)
        if t == 0:
            total = total * SCALE
        kv_out[t] = total.astype(BF16)

    for i in range(4):
        own_out(i).start()
    for k in range(1, NH):
        for i in range(2):
            kv_back(k, i).start()

    back_one = [[[], []], [[], []]]
    back_z = []

    def merge_rolls(t, p):
        o_z = zh if p == 0 else 1 - zh

        def merge(a, _):
            o = at(t, a, place[1 - t], o_z)
            low = high = jnp.zeros((BLOCK, HD), F32)
            for b in range(size[1 - t]):
                pr = par_ref[o, at(t, place[t], b, zh)]
                m = gr[t, p, b, a].astype(F32)
                low = low + m * (1.0 - pr)
                high = high + m * pr
            s1[t, p, a, 0:BLOCK] = low.astype(BF16)
            s1[t, p, a, BLOCK : 2 * BLOCK] = high.astype(BF16)
            return 0

        lax.fori_loop(0, size[t], merge, 0)

    for p in (1, 0):
        for t in range(2):
            for c in back_two[t][p]:
                c.wait_recv()
            merge_rolls(t, p)
            for d in range(1, size[t]):
                a = lax.rem(place[t] + d, size[t])
                c = remote(
                    s1.at[t, p, a], r1.at[t, p, place[t]],
                    one_bs.at[t, p, d], one_br.at[t, p, d], first(t, d),
                )
                c.start()
                back_one[t][p].append(c)
            r1[t, p, place[t]] = s1[t, p, place[t]]
        if p == 1:
            lax.fori_loop(MIDDLE, STEPS, send_back, 0)
        for t in range(2):
            for c in back_one[t][p]:
                c.wait_recv()
            total = r1[t, p, 0].astype(F32)
            for a in range(1, size[t]):
                total = total + r1[t, p, a].astype(F32)
            if p == 1:
                zs[t] = total.astype(BF16)
                c = remote(zs.at[t], zr.at[t], zb_s.at[t], zb_r.at[t], z_dev)
                c.start()
                back_z.append(c)
            else:
                back_z[t].wait_recv()
                (dkg_ref, dvg_ref)[t][...] = total + zr[t].astype(F32)

    for i in range(4):
        own_out(i).wait()
    for k in range(1, NH):
        for i in range(2):
            kv_copy(k, i).wait_send()
            kv_back(k, i).wait()

    def drain(j, _):
        for k in range(1, NH):
            for i in range(2):
                chunk_copy(k, i, j).wait_send()
                chunk_back(k, i, j).wait()
        return 0

    lax.fori_loop(0, STEPS, drain, 0)
    for c in z_copy + two + back_z:
        c.wait_send()
    for group in (one, back_two, back_one):
        for t in range(2):
            for p in range(2):
                for c in group[t][p]:
                    c.wait_send()


def copy_out(*refs):
    n = (len(refs) - 1) // 3
    src, dst, held, sem = refs[:n], refs[n : 2 * n], refs[2 * n : 3 * n], refs[-1]
    into = [pltpu.make_async_copy(src[i], held[i], sem.at[0, i]) for i in range(n)]
    back = [pltpu.make_async_copy(held[i], dst[i], sem.at[1, i]) for i in range(n)]
    for c in into:
        c.start()
    for i in range(n):
        into[i].wait()
        back[i].start()
    for c in back:
        c.wait()


def local(queries, keys, values, cotangent, doc_keys, doc_values, citations, block_lists):
    n = max(NX, NY)
    any_spec = pl.BlockSpec(memory_space=pltpu.HBM)
    vmem = pl.BlockSpec(memory_space=pltpu.VMEM)
    smem = pl.BlockSpec(memory_space=pltpu.SMEM)
    dma = pltpu.SemaphoreType.DMA
    blk = (BLOCK, HD)
    sd = jax.ShapeDtypeStruct
    results = pl.pallas_call(
        kernel,
        out_shape=(
            sd(queries.shape, BF16), sd(queries.shape, BF16), sd(keys.shape, BF16), sd(keys.shape, BF16),
            sd(doc_keys.shape, F32), sd(doc_keys.shape, F32),
        ),
        in_specs=[any_spec] * 6 + [vmem, smem, smem],
        out_specs=(any_spec,) * 4 + (vmem,) * 2,
        scratch_shapes=[
            pltpu.VMEM((QTOK, WIDE), BF16),
            pltpu.VMEM((QTOK, WIDE), BF16),
            pltpu.VMEM((QTOK, HD), BF16),
            pltpu.VMEM((QTOK, HD), BF16),
            pltpu.VMEM((2, 2, n, 2 * BLOCK, HD), BF16),
            pltpu.VMEM((2, 2, n - 1, n) + blk, BF16),
            pltpu.VMEM((2, 2 * n * n) + blk, BF16),
            pltpu.VMEM((2, 2, KEYS, HD), BF16),
            pltpu.VMEM((2, 2, HD, KEYS), BF16),
            pltpu.VMEM((2, 2, NONE + 1) + blk, F32),
            pltpu.VMEM((QTOK, WIDE), BF16),
            pltpu.VMEM((QTOK, WIDE), BF16),
            pltpu.VMEM((2, QTOK, HD), BF16),
            pltpu.VMEM((2, 2, n, n) + blk, BF16),
            pltpu.VMEM((2, 2, n, n) + blk, BF16),
            pltpu.VMEM((2, 2, n, 2 * BLOCK, HD), BF16),
            pltpu.VMEM((2, 2, n, 2 * BLOCK, HD), BF16),
            pltpu.VMEM((2, 2 * BLOCK, HD), BF16),
            pltpu.VMEM((2, 2 * BLOCK, HD), BF16),
            pltpu.VMEM((2 * NX * NY, HD), F32),
            pltpu.SMEM((2 * NX * NY, HD), F32),
            dma((1,)),
            dma((4,)), dma((2,)), dma((NH, 2)), dma((NH, 2)), dma((NH, 2, STEPS)), dma((NH, 2, STEPS)),
            dma((2,)), dma((2,)),
            dma((2, 2, n)), dma((2, 2, n)), dma((2, 2, n)), dma((2, 2, n)),
            dma((NH, 2)), dma((NH, 2)), dma((NH, 2, STEPS)), dma((NH, 2, STEPS)), dma((4,)),
            dma((2, 2, n)), dma((2, 2, n)), dma((2, 2, n)), dma((2, 2, n)), dma((2,)), dma((2,)),
        ],
        compiler_params=pltpu.CompilerParams(
            collective_id=0, has_side_effects=True, vmem_limit_bytes=60 * 2**20
        ),
        name="attention",
    )(queries, cotangent, keys, values, doc_keys, doc_values, citations.T, citations.T, block_lists)
    return pl.pallas_call(
        copy_out,
        out_shape=tuple(sd(r.shape, r.dtype) for r in results),
        in_specs=[any_spec] * 6,
        out_specs=(any_spec,) * 6,
        scratch_shapes=[pltpu.VMEM(r.shape, r.dtype) for r in results] + [dma((2, 6))],
        compiler_params=pltpu.CompilerParams(vmem_limit_bytes=60 * 2**20),
        name="copy_out",
    )(*results)


def solution(mesh):
    return jax.shard_map(
        local,
        mesh=mesh,
        in_specs=(
            P(("roll", "head"), None),
            P(("roll", "head"), None),
            P(("roll", "head"), None),
            P(("roll", "head"), None),
            P("roll", "head"),
            P("roll", "head"),
            P(),
            P("roll", None),
        ),
        out_specs=(
            P(("roll", "head"), None),
            P(("roll", "head"), None),
            P(("roll", "head"), None),
            P(("roll", "head"), None),
            P("roll", "head"),
            P("roll", "head"),
        ),
        check_vma=False,
    )
```

```python
import functools
import math

import jax
import jax.numpy as jnp
from jax import lax
from jax.experimental import pallas as pl
from jax.experimental.pallas import tpu as pltpu
from jax.sharding import PartitionSpec as P

HD = 128
BLOCK = 128
GROUP = 8
LIST = 4
QTOK = 256
NX = 4
NY = 4
NH = 8
WIDE = GROUP * HD
ROWS = QTOK // NH
KEYS = LIST * BLOCK + QTOK
NONE = KEYS // BLOCK
PAIR = 2 * HD
STEPS = GROUP // 2
CUTS = (2, 3, 4, 4)
LAG = 1
VMEM_MIB = 56
ORDER_OUT = (4, 3, 5, 2, 6, 1, 7)
MESH = pl.DeviceIdType.MESH
SCALE = 1.0 / math.sqrt(HD)
LOG2E = math.log2(math.e)
F32 = jnp.float32
BF16 = jnp.bfloat16


def roll_of(x, y, z):
    return (y * 2 + z) * NX + x


def dot(a, b, ca, cb):
    return lax.dot_general(a, b, (((ca,), (cb,)), ((), ())), preferred_element_type=F32)


def kernel(
    q_ref, g_ref, k_ref, v_ref, dk_ref, dv_ref, cite_v_ref, cite_ref, list_ref,
    att_ref, qg_ref, kg_ref, vg_ref, dkg_ref, dvg_ref,
    qw, gw, kw, vw, ag, sel, pool, cat, cat_t, acc, att, dq, kv_out, gs, gr, s1, r1, zs, zr,
    par_v, par_ref, pos_ref, par_sem, own_q, own_doc, kv_s, kv_r, head_s, head_r, z_s, z_r, one_s, one_r, two_s, two_r,
    kvo_s, kvo_r, out_s, out_r, out_l, two_bs, two_br, one_bs, one_br, zb_s, zb_r,
):
    roll = lax.axis_index("roll")
    head = lax.axis_index("head")
    x = lax.rem(roll, NX)
    zh = lax.rem(roll // NX, 2)
    y = roll // (2 * NX)
    z_dev = (roll_of(x, y, 1 - zh), head)

    place = (x, y)
    size = (NX, NY)
    docs = (dk_ref, dv_ref)

    def at(t, a, b, z):
        return roll_of(a, b, z) if t == 0 else roll_of(b, a, z)

    def first(t, d):
        a = lax.rem(place[t] + d, size[t])
        return (at(t, a, place[1 - t], zh), head)

    def second(t, d):
        b = lax.rem(place[1 - t] + d, size[1 - t])
        return (at(t, place[t], b, zh), head)

    def remote(src, dst, ss, rs, dev):
        return pltpu.make_async_remote_copy(
            src_ref=src, dst_ref=dst, send_sem=ss, recv_sem=rs, device_id=dev, device_id_type=MESH
        )

    def landed(ref, sem):
        pltpu.make_async_copy(ref, ref, sem).wait()

    barrier = pltpu.get_barrier_semaphore()
    partners = [z_dev]
    partners += [first(t, d) for t in range(2) for d in range(1, size[t])]
    partners += [(roll, lax.rem(head + k, NH)) for k in range(1, NH)]
    for dev in partners:
        pl.semaphore_signal(barrier, inc=1, device_id=dev, device_id_type=MESH)

    pl.semaphore_wait(barrier, len(partners))

    z_copy = []
    for t in range(2):
        c = remote(docs[t], ag.at[t, 1, place[t]], z_s.at[t], z_r.at[t], z_dev)
        c.start()
        z_copy.append(c)
    for t in range(2):
        for d in range(1, size[t]):
            c = remote(
                docs[t], ag.at[t, 0, place[t]], one_s.at[t, 0], one_r.at[t, 0], first(t, d)
            )
            c.start()
    own_docs = []
    for t in range(2):
        c = pltpu.make_async_copy(docs[t], ag.at[t, 0, place[t]], own_doc.at[t])
        c.start()
        own_docs.append(c)
    heads = []
    mine = pl.ds(pl.multiple_of(head * ROWS, ROWS), ROWS)
    moved = ((k_ref, kw, HD), (v_ref, vw, HD), (q_ref, qw, WIDE), (g_ref, gw, WIDE))
    for i, (src, dst, width) in enumerate(moved):
        c = pltpu.make_async_copy(
            src.at[:, pl.ds(pl.multiple_of(head * width, width), width)], dst.at[mine], own_q.at[i]
        )
        c.start()
        heads.append(c)

    def kv_copy(k, i):
        h = lax.rem(head + k, NH)
        src, dst, width = moved[i]
        return remote(
            src.at[:, pl.ds(pl.multiple_of(h * width, width), width)],
            dst.at[mine], kv_s.at[i], kv_r.at[i], (roll, h),
        )

    def chunk_copy(k, i, j):
        h = lax.rem(head + k, NH)
        src, dst, width = moved[2 + i]
        return remote(
            src.at[:, pl.ds(pl.multiple_of(h * width + j * PAIR, PAIR), PAIR)],
            dst.at[mine, pl.ds(pl.multiple_of(j * PAIR, PAIR), PAIR)],
            head_s.at[i], head_r.at[i, j], (roll, h),
        )

    for k in range(1, NH):
        for i in range(2):
            kv_copy(k, i).start()

    def send_chunks(j, _):
        for k in range(1, NH):
            for i in range(2):
                chunk_copy(k, i, j).start()
        return 0

    lax.fori_loop(0, STEPS, send_chunks, 0)

    cites = cite_v_ref[...]
    rolls = 2 * NX * NY
    owner_at = lax.broadcasted_iota(jnp.int32, (rolls, rolls), 0)
    odd = jnp.zeros((rolls, rolls), jnp.int32)
    for c in range(cites.shape[0]):
        cite = cites[c : c + 1]
        odd = odd + jnp.where((cite >> 1) == owner_at, cite & 1, 0)

    par_v[:, 0:rolls] = odd.astype(F32)
    par_copy = pltpu.make_async_copy(par_v, par_ref, par_sem.at[0])
    par_copy.start()
    acc[...] = jnp.zeros_like(acc)
    par_copy.wait()

    owners = [[cite_ref[list_ref[b, i], roll] >> 1 for i in range(LIST)] for b in range(2)]

    def find(o, _):
        for b in range(2):
            found = jnp.int32(NONE)
            for i in range(LIST):
                same = (owners[b][i] == o).astype(jnp.int32)
                found = found + same * (i - found)
            pos_ref[b, o] = found
        return 0

    lax.fori_loop(0, rolls, find, 0)

    def slot(t, p, b, a):
        return (p * size[1 - t] + b) * size[t] + a

    def pick(t, p):
        o_z = zh if p == 0 else 1 - zh
        for d in range(size[1 - t]):
            target = second(t, d)[0]

            def step(a, _):
                pr = par_ref[at(t, a, place[1 - t], o_z), target]
                low = ag[t, p, a, 0:BLOCK].astype(F32)
                high = ag[t, p, a, BLOCK : 2 * BLOCK].astype(F32)
                chosen = (low * (1.0 - pr) + high * pr).astype(BF16)
                if d == 0:
                    pool[t, slot(t, p, place[1 - t], a)] = chosen
                else:
                    sel[t, p, d - 1, a] = chosen
                return 0

            lax.fori_loop(0, size[t], step, 0)

    for p in range(2):
        if p == 1:
            for t in range(2):
                z_copy[t].wait_recv()
                for d in range(1, size[t]):
                    c = remote(
                        ag.at[t, 1, place[t]], ag.at[t, 1, place[t]],
                        one_s.at[t, 1], one_r.at[t, 1], first(t, d),
                    )
                    c.start()
        for t in range(2):
            if p == 0:
                own_docs[t].wait()
            landed(ag.at[t, p, 0 : size[t] - 1], one_r.at[t, p])
            pick(t, p)
            for d in range(1, size[1 - t]):
                c = remote(
                    sel.at[t, p, d - 1], pool.at[t, pl.ds(slot(t, p, place[1 - t], 0), size[t])],
                    two_s.at[t, p], two_r.at[t, p], second(t, d),
                )
                c.start()
    for c in heads:
        c.wait()
    others = QTOK - ROWS
    for i, ref in enumerate((kw, vw)):
        landed(ref.at[0:others], kv_r.at[i])
    for t in range(2):
        for p in range(2):
            landed(pool.at[t, 0 : (size[1 - t] - 1) * size[t]], two_r.at[t, p])

    for b in range(2):
        for i in range(LIST):
            o = owners[b][i]
            ox, oz, oy = o & (NX - 1), (o // NX) & 1, o // (2 * NX)
            slots = [((oz ^ zh) * NY + oy) * NX + ox, ((oz ^ zh) * NX + ox) * NY + oy]
            rows = pl.ds(i * BLOCK, BLOCK)
            for t in range(2):
                cat[t, b, rows] = pool[t, slots[t]]
        cat[0, b, LIST * BLOCK : KEYS] = kw[...]
        cat[1, b, LIST * BLOCK : KEYS] = vw[...]
        for t in range(2):
            cat_t[t, b] = cat[t, b].T

    def compute(b, j):
        c0 = pl.multiple_of(j * PAIR, PAIR)
        c1 = pl.multiple_of(c0 + HD, HD)
        rows = pl.ds(pl.multiple_of(b * BLOCK, BLOCK), BLOCK)
        cols = (pl.ds(c0, HD), pl.ds(c1, HD))
        query = jnp.concatenate([qw[rows, c] for c in cols], axis=0)
        grad = jnp.concatenate([gw[rows, c] for c in cols], axis=0)
        score = dot(cat[0, b], query, 1, 1)
        local = score[LIST * BLOCK :]
        key_at = lax.broadcasted_iota(jnp.int32, local.shape, 0)
        query_at = lax.rem(lax.broadcasted_iota(jnp.int32, local.shape, 1), BLOCK) + b * BLOCK
        local = jnp.where(key_at <= query_at, local, -jnp.inf)
        score = jnp.concatenate([score[: LIST * BLOCK], local], axis=0)
        top = jnp.max(score, axis=0, keepdims=True)
        e = jnp.exp2((score - top) * (SCALE * LOG2E))
        prob = e * (1.0 / jnp.sum(e, axis=0, keepdims=True))
        weight = prob.astype(BF16)
        dprob = dot(cat[1, b], grad, 1, 1)
        delta = jnp.sum(prob * dprob, axis=0, keepdims=True)
        dscore = (prob * (dprob - delta)).astype(BF16)
        acc[1, b, 0:NONE] += dot(weight, grad, 1, 0).reshape(NONE, BLOCK, HD)
        acc[0, b, 0:NONE] += dot(dscore, query, 1, 0).reshape(NONE, BLOCK, HD)
        out_t = dot(cat_t[1, b], weight, 1, 0)
        dq_t = dot(cat_t[0, b], dscore, 1, 0) * SCALE
        for i, c in enumerate(cols):
            att[rows, c] = out_t[:, i * HD : (i + 1) * HD].T.astype(BF16)
            dq[rows, c] = dq_t[:, i * HD : (i + 1) * HD].T.astype(BF16)

    back = ((att, att_ref, WIDE), (dq, qg_ref, WIDE), (kv_out.at[0], kg_ref, HD), (kv_out.at[1], vg_ref, HD))

    def own_out(i):
        src, dst, width = back[i]
        there = pl.ds(pl.multiple_of(head * width, width), width)
        return pltpu.make_async_copy(src.at[mine], dst.at[:, there], out_l.at[i])

    def kv_back(k, i):
        h = lax.rem(head + k, NH)
        src, dst, width = back[2 + i]
        theirs = pl.ds(pl.multiple_of(h * ROWS, ROWS), ROWS)
        there = pl.ds(pl.multiple_of(head * width, width), width)
        return remote(src.at[theirs], dst.at[:, there], kvo_s.at[i], kvo_r.at[i], (roll, h))

    def chunk_back(k, i, j):
        h = lax.rem(head + k, NH)
        src, dst, width = back[i]
        theirs = pl.ds(pl.multiple_of(h * ROWS, ROWS), ROWS)
        return remote(
            src.at[theirs, pl.ds(pl.multiple_of(j * PAIR, PAIR), PAIR)],
            dst.at[:, pl.ds(pl.multiple_of(head * width + j * PAIR, PAIR), PAIR)],
            out_s.at[i], out_r.at[i], (roll, h),
        )

    def send_back(j, _):
        for k in ORDER_OUT:
            for i in range(2):
                chunk_back(k, i, j).start()
        return 0

    def per_chunk(j, _):
        for i, ref in enumerate((qw, gw)):
            landed(ref.at[0:others, pl.ds(pl.multiple_of(j * PAIR, PAIR), PAIR)], head_r.at[i, j])

        def per_block(b, _):
            compute(b, j)
            return 0

        lax.fori_loop(0, 2, per_block, 0)
        @pl.when((j >= LAG) & (j < CUTS[0] + LAG))
        def _():
            send_back(j - LAG, 0)

        return 0

    lax.fori_loop(0, STEPS, per_chunk, 0)

    def prepare(t, p, b):
        def step(a, _):
            o = at(t, a, b, zh if p == 0 else 1 - zh)
            total = acc[t, 0, pos_ref[0, o]] + acc[t, 1, pos_ref[1, o]]
            if t == 0:
                total = total * SCALE
            gs[t, p, b, a] = total.astype(BF16)

        for a in range(size[t]):
            step(a, 0)

    for p in (1, 0):
        for d in range(1, NX):
            for t in range(2):
                b = lax.rem(place[1 - t] + d, size[1 - t])
                prepare(t, p, b)
                c = remote(
                    gs.at[t, p, b], gr.at[t, p, place[1 - t]],
                    two_bs.at[t, p], two_br.at[t, p], second(t, d),
                )
                c.start()
    lax.fori_loop(CUTS[0], CUTS[1], send_back, 0)
    for p in (1, 0):
        for t in range(2):
            b = place[1 - t]
            prepare(t, p, b)
            gr[t, p, b] = gs[t, p, b]

    for t in range(2):
        total = (acc[t, 0, LIST:NONE] + acc[t, 1, LIST:NONE]).reshape(QTOK, HD)
        if t == 0:
            total = total * SCALE
        kv_out[t] = total.astype(BF16)

    for i in range(4):
        own_out(i).start()
    for k in range(1, NH):
        for i in range(2):
            kv_back(k, i).start()

    back_z = []

    def merge_rolls(t, p):
        o_z = zh if p == 0 else 1 - zh

        def merge(a, _):
            o = at(t, a, place[1 - t], o_z)
            low = high = jnp.zeros((BLOCK, HD), F32)
            for b in range(size[1 - t]):
                pr = par_ref[o, at(t, place[t], b, zh)]
                m = gr[t, p, b, a].astype(F32)
                low = low + m * (1.0 - pr)
                high = high + m * pr
            s1[t, p, a, 0:BLOCK] = low.astype(BF16)
            s1[t, p, a, BLOCK : 2 * BLOCK] = high.astype(BF16)
            return 0

        lax.fori_loop(0, size[t], merge, 0)

    for p in (1, 0):
        if p == 0:
            lax.fori_loop(CUTS[2], CUTS[3], send_back, 0)
            for c in z_copy:
                c.wait_send()
            for i, ref in enumerate((kw, vw)):
                landed(ref.at[0:others], kv_s.at[i])
            for i, ref in enumerate((qw, gw)):
                landed(ref.at[0:others], head_s.at[i])
            for t in range(2):
                for q in range(2):
                    landed(ag.at[t, q, 0 : size[t] - 1], one_s.at[t, q])
                    landed(sel.at[t, q], two_s.at[t, q])
                landed(gs.at[t, 1, 0 : size[1 - t] - 1], two_bs.at[t, 1])
            for i in range(4):
                own_out(i).wait()
        for t in range(2):
            landed(gr.at[t, p, 0 : size[1 - t] - 1], two_br.at[t, p])
            merge_rolls(t, p)
            for d in range(1, size[t]):
                a = lax.rem(place[t] + d, size[t])
                c = remote(
                    s1.at[t, p, a], r1.at[t, p, place[t]],
                    one_bs.at[t, p], one_br.at[t, p], first(t, d),
                )
                c.start()
            r1[t, p, place[t]] = s1[t, p, place[t]]
        if p == 1:
            lax.fori_loop(CUTS[1], CUTS[2], send_back, 0)
        for t in range(2):
            landed(r1.at[t, p, 0 : size[t] - 1], one_br.at[t, p])
            total = r1[t, p, 0].astype(F32)
            for a in range(1, size[t]):
                total = total + r1[t, p, a].astype(F32)
            if p == 1:
                zs[t] = total.astype(BF16)
                c = remote(zs.at[t], zr.at[t], zb_s.at[t], zb_r.at[t], z_dev)
                c.start()
                back_z.append(c)
            else:
                if t == 0:
                    lax.fori_loop(CUTS[3], STEPS, send_back, 0)
                    for i in range(2):
                        for u in range(2):
                            landed(r1.at[u, i, 0 : size[u] - 1], one_bs.at[u, i])
                        landed(gs.at[i, 0, 0 : size[1 - i] - 1], two_bs.at[i, 0])
                        landed(kg_ref.at[:, 0 : HD * (NH - 1)], kvo_r.at[i])
                        landed(kv_out.at[i, 0:others], kvo_s.at[i])
                        landed(att.at[0:others], out_s.at[i])
                back_z[t].wait_recv()
                (dkg_ref, dvg_ref)[t][...] = total + zr[t].astype(F32)

    for i in range(2):
        landed(att_ref.at[:, 0 : WIDE * (NH - 1)], out_r.at[i])
    for c in back_z:
        c.wait_send()


def copy_out(*refs):
    n = len(refs) // 2
    copies = [pltpu.make_async_copy(refs[i], refs[n + i], refs[-1].at[i]) for i in range(n)]
    for c in copies:
        c.start()
    for c in copies:
        c.wait()


def local(queries, keys, values, cotangent, doc_keys, doc_values, citations, block_lists):
    n = max(NX, NY)
    any_spec = pl.BlockSpec(memory_space=pltpu.HBM)
    vmem = pl.BlockSpec(memory_space=pltpu.VMEM)
    smem = pl.BlockSpec(memory_space=pltpu.SMEM)
    dma = pltpu.SemaphoreType.DMA
    blk = (BLOCK, HD)
    sd = jax.ShapeDtypeStruct
    results = pl.pallas_call(
        kernel,
        out_shape=(
            pltpu.VMEM(queries.shape, BF16), pltpu.VMEM(queries.shape, BF16),
            pltpu.VMEM(keys.shape, BF16), pltpu.VMEM(keys.shape, BF16),
            pltpu.VMEM(doc_keys.shape, F32), pltpu.VMEM(doc_keys.shape, F32),
        ),
        in_specs=[any_spec] * 6 + [vmem, smem, smem],
        out_specs=(vmem,) * 6,
        scratch_shapes=[
            pltpu.VMEM((QTOK, WIDE), BF16),
            pltpu.VMEM((QTOK, WIDE), BF16),
            pltpu.VMEM((QTOK, HD), BF16),
            pltpu.VMEM((QTOK, HD), BF16),
            pltpu.VMEM((2, 2, n, 2 * BLOCK, HD), BF16),
            pltpu.VMEM((2, 2, n - 1, n) + blk, BF16),
            pltpu.VMEM((2, 2 * n * n) + blk, BF16),
            pltpu.VMEM((2, 2, KEYS, HD), BF16),
            pltpu.VMEM((2, 2, HD, KEYS), BF16),
            pltpu.VMEM((2, 2, NONE + 1) + blk, F32),
            pltpu.VMEM((QTOK, WIDE), BF16),
            pltpu.VMEM((QTOK, WIDE), BF16),
            pltpu.VMEM((2, QTOK, HD), BF16),
            pltpu.VMEM((2, 2, n, n) + blk, BF16),
            pltpu.VMEM((2, 2, n, n) + blk, BF16),
            pltpu.VMEM((2, 2, n, 2 * BLOCK, HD), BF16),
            pltpu.VMEM((2, 2, n, 2 * BLOCK, HD), BF16),
            pltpu.VMEM((2, 2 * BLOCK, HD), BF16),
            pltpu.VMEM((2, 2 * BLOCK, HD), BF16),
            pltpu.VMEM((2 * NX * NY, HD), F32),
            pltpu.SMEM((2 * NX * NY, HD), F32),
            pltpu.SMEM((2, 2 * NX * NY), jnp.int32),
            dma((1,)),
            dma((4,)), dma((2,)), dma((2,)), dma((2,)), dma((2,)), dma((2, STEPS)),
            dma((2,)), dma((2,)),
            dma((2, 2)), dma((2, 2)), dma((2, 2)), dma((2, 2)),
            dma((2,)), dma((2,)), dma((2,)), dma((2,)), dma((4,)),
            dma((2, 2)), dma((2, 2)), dma((2, 2)), dma((2, 2)), dma((2,)), dma((2,)),
        ],
        compiler_params=pltpu.CompilerParams(
            collective_id=0, has_side_effects=True, vmem_limit_bytes=VMEM_MIB * 2**20
        ),
        name="attention",
    )(*[pltpu.with_memory_space_constraint(r, pltpu.HBM) for r in (queries, cotangent, keys, values, doc_keys, doc_values)], citations.T, citations.T, block_lists)
    return pl.pallas_call(
        copy_out,
        out_shape=tuple(sd(r.shape, r.dtype) for r in results),
        in_specs=[vmem] * 6,
        out_specs=(any_spec,) * 6,
        scratch_shapes=[dma((6,))],
        compiler_params=pltpu.CompilerParams(vmem_limit_bytes=VMEM_MIB * 2**20),
        name="copy_out",
    )(*[pltpu.with_memory_space_constraint(r, pltpu.VMEM) for r in results])


def solution(mesh):
    return jax.shard_map(
        local,
        mesh=mesh,
        in_specs=(
            P(("roll", "head"), None),
            P(("roll", "head"), None),
            P(("roll", "head"), None),
            P(("roll", "head"), None),
            P("roll", "head"),
            P("roll", "head"),
            P(),
            P("roll", None),
        ),
        out_specs=(
            P(("roll", "head"), None),
            P(("roll", "head"), None),
            P(("roll", "head"), None),
            P(("roll", "head"), None),
            P("roll", "head"),
            P("roll", "head"),
        ),
        check_vma=False,
    )
```

```python
import functools
import math

import jax
import jax.numpy as jnp
from jax import lax
from jax.experimental import pallas as pl
from jax.experimental.pallas import tpu as pltpu
from jax.sharding import PartitionSpec as P

HD = 128
BLOCK = 128
GROUP = 8
LIST = 4
QTOK = 256
NX = 4
NY = 4
NH = 8
WIDE = GROUP * HD
ROWS = QTOK // NH
KEYS = LIST * BLOCK + QTOK
NONE = KEYS // BLOCK
PAIR = 2 * HD
STEPS = GROUP // 2
CUTS = (2, 3, 4, 4)
LAG = 1
VMEM_MIB = 56
FIRST = 1
ORDER_OUT = (1, 2, 3, 4, 5, 6, 7)
MESH = pl.DeviceIdType.MESH
SCALE = 1.0 / math.sqrt(HD)
LOG2E = math.log2(math.e)
F32 = jnp.float32
BF16 = jnp.bfloat16


def roll_of(x, y, z):
    return (y * 2 + z) * NX + x


def dot(a, b, ca, cb):
    return lax.dot_general(a, b, (((ca,), (cb,)), ((), ())), preferred_element_type=F32)


def kernel(
    q_ref, g_ref, k_ref, v_ref, dk_ref, dv_ref, cite_hbm, list_hbm,
    att_ref, qg_ref, kg_ref, vg_ref, dkg_ref, dvg_ref,
    qw, gw, kw, vw, ag, sel, pool, cat, cat_t, acc, att, dq, kv_out, gs, gr, s1, r1, zs, zr,
    open_sem, cite_v_ref, cite_ref, list_ref, small_sem, par_v, par_ref, pos_ref, par_sem, own_q, own_doc, kv_s, kv_r, head_s, head_r, z_s, z_r, one_s, one_r, two_s, two_r,
    kvo_s, kvo_r, out_s, out_r, out_l, two_bs, two_br, one_bs, one_br, zb_s, zb_r,
):
    roll = lax.axis_index("roll")
    head = lax.axis_index("head")
    x = lax.rem(roll, NX)
    zh = lax.rem(roll // NX, 2)
    y = roll // (2 * NX)
    z_dev = (roll_of(x, y, 1 - zh), head)

    place = (x, y)
    size = (NX, NY)
    docs = (dk_ref, dv_ref)

    def at(t, a, b, z):
        return roll_of(a, b, z) if t == 0 else roll_of(b, a, z)

    def first(t, d):
        a = lax.rem(place[t] + d, size[t])
        return (at(t, a, place[1 - t], zh), head)

    def second(t, d):
        b = lax.rem(place[1 - t] + d, size[1 - t])
        return (at(t, place[t], b, zh), head)

    def remote(src, dst, ss, rs, dev):
        return pltpu.make_async_remote_copy(
            src_ref=src, dst_ref=dst, send_sem=ss, recv_sem=rs, device_id=dev, device_id_type=MESH
        )

    def landed(ref, sem):
        pltpu.make_async_copy(ref, ref, sem).wait()

    barrier = pltpu.get_barrier_semaphore()
    partners = [first(t, d) for t in range(2) for d in range(1, size[t])]
    partners += [(roll, lax.rem(head + k, NH)) for k in range(1, NH)]
    for dev in partners:
        pl.semaphore_signal(barrier, inc=1, device_id=dev, device_id_type=MESH)
    small = [
        pltpu.make_async_copy(cite_hbm, cite_v_ref, small_sem.at[0]),
        pltpu.make_async_copy(cite_hbm, cite_ref, small_sem.at[1]),
        pltpu.make_async_copy(list_hbm, list_ref, small_sem.at[2]),
    ]
    for c in small:
        c.start()
    gate, other_gate = (NH - 1) * (1 - zh), (NH - 1) * zh
    pl.semaphore_signal(
        barrier, inc=1, device_id=(roll_of(x, y, 1 - zh), other_gate), device_id_type=MESH
    )

    @pl.when(head == gate)
    def _():
        pl.semaphore_wait(barrier, len(partners) + NH)
        for k in range(1, NH):
            pl.semaphore_signal(
                open_sem, inc=1, device_id=(roll, lax.rem(head + k, NH)), device_id_type=MESH
            )

    @pl.when(head != gate)
    def _():
        pl.semaphore_wait(barrier, len(partners))

    for t in range(2):
        for d in range(1, size[t]):
            c = remote(
                docs[t], ag.at[t, 0, place[t]], one_s.at[t, 0], one_r.at[t, 0], first(t, d)
            )
            c.start()
    own_docs = []
    for t in range(2):
        c = pltpu.make_async_copy(docs[t], ag.at[t, 0, place[t]], own_doc.at[t])
        c.start()
        own_docs.append(c)
    heads = []
    mine = pl.ds(pl.multiple_of(head * ROWS, ROWS), ROWS)
    moved = ((k_ref, kw, HD), (v_ref, vw, HD), (q_ref, qw, WIDE), (g_ref, gw, WIDE))
    for i, (src, dst, width) in enumerate(moved):
        c = pltpu.make_async_copy(
            src.at[:, pl.ds(pl.multiple_of(head * width, width), width)], dst.at[mine], own_q.at[i]
        )
        c.start()
        heads.append(c)

    def kv_copy(k, i):
        h = lax.rem(head + k, NH)
        src, dst, width = moved[i]
        return remote(
            src.at[:, pl.ds(pl.multiple_of(h * width, width), width)],
            dst.at[mine], kv_s.at[i], kv_r.at[i], (roll, h),
        )

    def chunk_copy(k, i, j):
        h = lax.rem(head + k, NH)
        src, dst, width = moved[2 + i]
        return remote(
            src.at[:, pl.ds(pl.multiple_of(h * width + j * PAIR, PAIR), PAIR)],
            dst.at[mine, pl.ds(pl.multiple_of(j * PAIR, PAIR), PAIR)],
            head_s.at[i], head_r.at[i, j], (roll, h),
        )

    for k in range(1, NH):
        for i in range(2):
            kv_copy(k, i).start()

    def send_chunks(j, _):
        for k in range(1, NH):
            for i in range(2):
                chunk_copy(k, i, j).start()
        return 0

    lax.fori_loop(0, FIRST, send_chunks, 0)

    @pl.when(head != gate)
    def _():
        pl.semaphore_wait(open_sem, 1)

    z_copy = []
    for t in range(2):
        c = remote(docs[t], ag.at[t, 1, place[t]], z_s.at[t], z_r.at[t], z_dev)
        c.start()
        z_copy.append(c)
    lax.fori_loop(FIRST, STEPS, send_chunks, 0)

    for c in small:
        c.wait()
    cites = cite_v_ref[...]
    rolls = 2 * NX * NY
    owner_at = lax.broadcasted_iota(jnp.int32, (rolls, rolls), 0)
    odd = jnp.zeros((rolls, rolls), jnp.int32)
    for c in range(cites.shape[0]):
        cite = cites[c : c + 1]
        odd = odd + jnp.where((cite >> 1) == owner_at, cite & 1, 0)

    par_v[:, 0:rolls] = odd.astype(F32)
    par_copy = pltpu.make_async_copy(par_v, par_ref, par_sem.at[0])
    par_copy.start()
    acc[...] = jnp.zeros_like(acc)
    par_copy.wait()

    owners = [[cite_ref[list_ref[b, i], roll] >> 1 for i in range(LIST)] for b in range(2)]

    def find(o, _):
        for b in range(2):
            found = jnp.int32(NONE)
            for i in range(LIST):
                same = (owners[b][i] == o).astype(jnp.int32)
                found = found + same * (i - found)
            pos_ref[b, o] = found
        return 0

    lax.fori_loop(0, rolls, find, 0)

    def slot(t, p, b, a):
        return (p * size[1 - t] + b) * size[t] + a

    def pick(t, p):
        o_z = zh if p == 0 else 1 - zh
        for d in range(size[1 - t]):
            target = second(t, d)[0]

            def step(a, _):
                pr = par_ref[at(t, a, place[1 - t], o_z), target]
                low = ag[t, p, a, 0:BLOCK].astype(F32)
                high = ag[t, p, a, BLOCK : 2 * BLOCK].astype(F32)
                chosen = (low * (1.0 - pr) + high * pr).astype(BF16)
                if d == 0:
                    pool[t, slot(t, p, place[1 - t], a)] = chosen
                else:
                    sel[t, p, d - 1, a] = chosen
                return 0

            lax.fori_loop(0, size[t], step, 0)

    for p in range(2):
        if p == 1:
            for t in range(2):
                z_copy[t].wait_recv()
                for d in range(1, size[t]):
                    c = remote(
                        ag.at[t, 1, place[t]], ag.at[t, 1, place[t]],
                        one_s.at[t, 1], one_r.at[t, 1], first(t, d),
                    )
                    c.start()
        for t in range(2):
            if p == 0:
                own_docs[t].wait()
            landed(ag.at[t, p, 0 : size[t] - 1], one_r.at[t, p])
            pick(t, p)
            for d in range(1, size[1 - t]):
                c = remote(
                    sel.at[t, p, d - 1], pool.at[t, pl.ds(slot(t, p, place[1 - t], 0), size[t])],
                    two_s.at[t, p], two_r.at[t, p], second(t, d),
                )
                c.start()
    for c in heads:
        c.wait()
    others = QTOK - ROWS
    for i, ref in enumerate((kw, vw)):
        landed(ref.at[0:others], kv_r.at[i])
    for t in range(2):
        for p in range(2):
            landed(pool.at[t, 0 : (size[1 - t] - 1) * size[t]], two_r.at[t, p])

    for b in range(2):
        for i in range(LIST):
            o = owners[b][i]
            ox, oz, oy = o & (NX - 1), (o // NX) & 1, o // (2 * NX)
            slots = [((oz ^ zh) * NY + oy) * NX + ox, ((oz ^ zh) * NX + ox) * NY + oy]
            rows = pl.ds(i * BLOCK, BLOCK)
            for t in range(2):
                cat[t, b, rows] = pool[t, slots[t]]
        cat[0, b, LIST * BLOCK : KEYS] = kw[...]
        cat[1, b, LIST * BLOCK : KEYS] = vw[...]
        for t in range(2):
            cat_t[t, b] = cat[t, b].T

    def compute(b, j):
        c0 = pl.multiple_of(j * PAIR, PAIR)
        c1 = pl.multiple_of(c0 + HD, HD)
        rows = pl.ds(pl.multiple_of(b * BLOCK, BLOCK), BLOCK)
        cols = (pl.ds(c0, HD), pl.ds(c1, HD))
        query = jnp.concatenate([qw[rows, c] for c in cols], axis=0)
        grad = jnp.concatenate([gw[rows, c] for c in cols], axis=0)
        score = dot(cat[0, b], query, 1, 1)
        local = score[LIST * BLOCK :]
        key_at = lax.broadcasted_iota(jnp.int32, local.shape, 0)
        query_at = lax.rem(lax.broadcasted_iota(jnp.int32, local.shape, 1), BLOCK) + b * BLOCK
        local = jnp.where(key_at <= query_at, local, -jnp.inf)
        score = jnp.concatenate([score[: LIST * BLOCK], local], axis=0)
        top = jnp.max(score, axis=0, keepdims=True)
        e = jnp.exp2((score - top) * (SCALE * LOG2E))
        prob = e * (1.0 / jnp.sum(e, axis=0, keepdims=True))
        weight = prob.astype(BF16)
        dprob = dot(cat[1, b], grad, 1, 1)
        delta = jnp.sum(prob * dprob, axis=0, keepdims=True)
        dscore = (prob * (dprob - delta)).astype(BF16)
        acc[1, b, 0:NONE] += dot(weight, grad, 1, 0).reshape(NONE, BLOCK, HD)
        acc[0, b, 0:NONE] += dot(dscore, query, 1, 0).reshape(NONE, BLOCK, HD)
        out_t = dot(cat_t[1, b], weight, 1, 0)
        dq_t = dot(cat_t[0, b], dscore, 1, 0) * SCALE
        for i, c in enumerate(cols):
            att[rows, c] = out_t[:, i * HD : (i + 1) * HD].T.astype(BF16)
            dq[rows, c] = dq_t[:, i * HD : (i + 1) * HD].T.astype(BF16)

    back = ((att, att_ref, WIDE), (dq, qg_ref, WIDE), (kv_out.at[0], kg_ref, HD), (kv_out.at[1], vg_ref, HD))

    def own_out(i):
        src, dst, width = back[i]
        there = pl.ds(pl.multiple_of(head * width, width), width)
        return pltpu.make_async_copy(src.at[mine], dst.at[:, there], out_l.at[i])

    def kv_back(k, i):
        h = lax.rem(head + k, NH)
        src, dst, width = back[2 + i]
        theirs = pl.ds(pl.multiple_of(h * ROWS, ROWS), ROWS)
        there = pl.ds(pl.multiple_of(head * width, width), width)
        return remote(src.at[theirs], dst.at[:, there], kvo_s.at[i], kvo_r.at[i], (roll, h))

    def chunk_back(k, i, j):
        h = lax.rem(head + k, NH)
        src, dst, width = back[i]
        theirs = pl.ds(pl.multiple_of(h * ROWS, ROWS), ROWS)
        return remote(
            src.at[theirs, pl.ds(pl.multiple_of(j * PAIR, PAIR), PAIR)],
            dst.at[:, pl.ds(pl.multiple_of(head * width + j * PAIR, PAIR), PAIR)],
            out_s.at[i], out_r.at[i], (roll, h),
        )

    def send_back(j, _):
        for k in ORDER_OUT:
            for i in range(2):
                chunk_back(k, i, j).start()
        return 0

    def per_chunk(j, _):
        for i, ref in enumerate((qw, gw)):
            landed(ref.at[0:others, pl.ds(pl.multiple_of(j * PAIR, PAIR), PAIR)], head_r.at[i, j])

        compute(0, j)
        compute(1, j)
        @pl.when((j >= LAG) & (j < CUTS[0] + LAG))
        def _():
            send_back(j - LAG, 0)

        return 0

    lax.fori_loop(0, STEPS, per_chunk, 0)

    def prepare(t, p, b):
        def step(a, _):
            o = at(t, a, b, zh if p == 0 else 1 - zh)
            total = acc[t, 0, pos_ref[0, o]] + acc[t, 1, pos_ref[1, o]]
            if t == 0:
                total = total * SCALE
            gs[t, p, b, a] = total.astype(BF16)

        for a in range(size[t]):
            step(a, 0)

    def send_two(p):
        for d in range(1, NX):
            for t in range(2):
                b = lax.rem(place[1 - t] + d, size[1 - t])
                prepare(t, p, b)
                c = remote(
                    gs.at[t, p, b], gr.at[t, p, place[1 - t]],
                    two_bs.at[t, p], two_br.at[t, p], second(t, d),
                )
                c.start()

    def own_two(p):
        for t in range(2):
            b = place[1 - t]
            prepare(t, p, b)
            gr[t, p, b] = gs[t, p, b]

    send_two(1)
    send_two(0)
    lax.fori_loop(CUTS[0], CUTS[1], send_back, 0)
    own_two(1)
    own_two(0)

    for t in range(2):
        total = (acc[t, 0, LIST:NONE] + acc[t, 1, LIST:NONE]).reshape(QTOK, HD)
        if t == 0:
            total = total * SCALE
        kv_out[t] = total.astype(BF16)

    for i in range(4):
        own_out(i).start()
    for k in range(1, NH):
        for i in range(2):
            kv_back(k, i).start()

    back_z = []

    def merge_rolls(t, p):
        o_z = zh if p == 0 else 1 - zh

        def merge(a, _):
            o = at(t, a, place[1 - t], o_z)
            low = high = jnp.zeros((BLOCK, HD), F32)
            for b in range(size[1 - t]):
                pr = par_ref[o, at(t, place[t], b, zh)]
                m = gr[t, p, b, a].astype(F32)
                low = low + m * (1.0 - pr)
                high = high + m * pr
            s1[t, p, a, 0:BLOCK] = low.astype(BF16)
            s1[t, p, a, BLOCK : 2 * BLOCK] = high.astype(BF16)
            return 0

        lax.fori_loop(0, size[t], merge, 0)

    for p in (1, 0):
        if p == 0:
            lax.fori_loop(CUTS[2], CUTS[3], send_back, 0)
            for c in z_copy:
                c.wait_send()
            for i, ref in enumerate((kw, vw)):
                landed(ref.at[0:others], kv_s.at[i])
            for i, ref in enumerate((qw, gw)):
                landed(ref.at[0:others], head_s.at[i])
            for t in range(2):
                for q in range(2):
                    landed(ag.at[t, q, 0 : size[t] - 1], one_s.at[t, q])
                    landed(sel.at[t, q], two_s.at[t, q])
                landed(gs.at[t, 1, 0 : size[1 - t] - 1], two_bs.at[t, 1])
            for i in range(4):
                own_out(i).wait()
        for t in range(2):
            landed(gr.at[t, p, 0 : size[1 - t] - 1], two_br.at[t, p])
            merge_rolls(t, p)
            for d in range(1, size[t]):
                a = lax.rem(place[t] + d, size[t])
                c = remote(
                    s1.at[t, p, a], r1.at[t, p, place[t]],
                    one_bs.at[t, p], one_br.at[t, p], first(t, d),
                )
                c.start()
            r1[t, p, place[t]] = s1[t, p, place[t]]
        if p == 1:
            lax.fori_loop(CUTS[1], CUTS[2], send_back, 0)
        for t in range(2):
            landed(r1.at[t, p, 0 : size[t] - 1], one_br.at[t, p])
            total = r1[t, p, 0].astype(F32)
            for a in range(1, size[t]):
                total = total + r1[t, p, a].astype(F32)
            if p == 1:
                zs[t] = total.astype(BF16)
                c = remote(zs.at[t], zr.at[t], zb_s.at[t], zb_r.at[t], z_dev)
                c.start()
                back_z.append(c)
            else:
                if t == 0:
                    lax.fori_loop(CUTS[3], STEPS, send_back, 0)
                    for i in range(2):
                        for u in range(2):
                            landed(r1.at[u, i, 0 : size[u] - 1], one_bs.at[u, i])
                        landed(gs.at[i, 0, 0 : size[1 - i] - 1], two_bs.at[i, 0])
                        landed(kg_ref.at[:, 0 : HD * (NH - 1)], kvo_r.at[i])
                        landed(kv_out.at[i, 0:others], kvo_s.at[i])
                        landed(att.at[0:others], out_s.at[i])
                back_z[t].wait_recv()
                (dkg_ref, dvg_ref)[t][...] = total + zr[t].astype(F32)

    for i in range(2):
        landed(att_ref.at[:, 0 : WIDE * (NH - 1)], out_r.at[i])
    for c in back_z:
        c.wait_send()


def copy_out(*refs):
    n = len(refs) // 2
    copies = [pltpu.make_async_copy(refs[i], refs[n + i], refs[-1].at[i]) for i in range(n)]
    for c in copies:
        c.start()
    for c in copies:
        c.wait()


def local(queries, keys, values, cotangent, doc_keys, doc_values, citations, block_lists):
    n = max(NX, NY)
    any_spec = pl.BlockSpec(memory_space=pltpu.HBM)
    vmem = pl.BlockSpec(memory_space=pltpu.VMEM)
    dma = pltpu.SemaphoreType.DMA
    blk = (BLOCK, HD)
    sd = jax.ShapeDtypeStruct
    results = pl.pallas_call(
        kernel,
        out_shape=(
            pltpu.VMEM(queries.shape, BF16), pltpu.VMEM(queries.shape, BF16),
            pltpu.VMEM(keys.shape, BF16), pltpu.VMEM(keys.shape, BF16),
            pltpu.VMEM(doc_keys.shape, F32), pltpu.VMEM(doc_keys.shape, F32),
        ),
        in_specs=[any_spec] * 8,
        out_specs=(vmem,) * 6,
        scratch_shapes=[
            pltpu.VMEM((QTOK, WIDE), BF16),
            pltpu.VMEM((QTOK, WIDE), BF16),
            pltpu.VMEM((QTOK, HD), BF16),
            pltpu.VMEM((QTOK, HD), BF16),
            pltpu.VMEM((2, 2, n, 2 * BLOCK, HD), BF16),
            pltpu.VMEM((2, 2, n - 1, n) + blk, BF16),
            pltpu.VMEM((2, 2 * n * n) + blk, BF16),
            pltpu.VMEM((2, 2, KEYS, HD), BF16),
            pltpu.VMEM((2, 2, HD, KEYS), BF16),
            pltpu.VMEM((2, 2, NONE + 1) + blk, F32),
            pltpu.VMEM((QTOK, WIDE), BF16),
            pltpu.VMEM((QTOK, WIDE), BF16),
            pltpu.VMEM((2, QTOK, HD), BF16),
            pltpu.VMEM((2, 2, n, n) + blk, BF16),
            pltpu.VMEM((2, 2, n, n) + blk, BF16),
            pltpu.VMEM((2, 2, n, 2 * BLOCK, HD), BF16),
            pltpu.VMEM((2, 2, n, 2 * BLOCK, HD), BF16),
            pltpu.VMEM((2, 2 * BLOCK, HD), BF16),
            pltpu.VMEM((2, 2 * BLOCK, HD), BF16),
            pltpu.SemaphoreType.REGULAR,
            pltpu.VMEM(citations.shape[::-1], jnp.int32),
            pltpu.SMEM(citations.shape[::-1], jnp.int32),
            pltpu.SMEM(block_lists.shape, jnp.int32),
            dma((3,)),
            pltpu.VMEM((2 * NX * NY, HD), F32),
            pltpu.SMEM((2 * NX * NY, HD), F32),
            pltpu.SMEM((2, 2 * NX * NY), jnp.int32),
            dma((1,)),
            dma((4,)), dma((2,)), dma((2,)), dma((2,)), dma((2,)), dma((2, STEPS)),
            dma((2,)), dma((2,)),
            dma((2, 2)), dma((2, 2)), dma((2, 2)), dma((2, 2)),
            dma((2,)), dma((2,)), dma((2,)), dma((2,)), dma((4,)),
            dma((2, 2)), dma((2, 2)), dma((2, 2)), dma((2, 2)), dma((2,)), dma((2,)),
        ],
        compiler_params=pltpu.CompilerParams(
            collective_id=0, has_side_effects=True, vmem_limit_bytes=VMEM_MIB * 2**20
        ),
        name="attention",
    )(*[pltpu.with_memory_space_constraint(r, pltpu.HBM) for r in (queries, cotangent, keys, values, doc_keys, doc_values, citations.T, block_lists)])
    return pl.pallas_call(
        copy_out,
        out_shape=tuple(sd(r.shape, r.dtype) for r in results),
        in_specs=[vmem] * 6,
        out_specs=(any_spec,) * 6,
        scratch_shapes=[dma((6,))],
        compiler_params=pltpu.CompilerParams(vmem_limit_bytes=VMEM_MIB * 2**20),
        name="copy_out",
    )(*[pltpu.with_memory_space_constraint(r, pltpu.VMEM) for r in results])


def solution(mesh):
    return jax.shard_map(
        local,
        mesh=mesh,
        in_specs=(
            P(("roll", "head"), None),
            P(("roll", "head"), None),
            P(("roll", "head"), None),
            P(("roll", "head"), None),
            P("roll", "head"),
            P("roll", "head"),
            P(),
            P("roll", None),
        ),
        out_specs=(
            P(("roll", "head"), None),
            P(("roll", "head"), None),
            P(("roll", "head"), None),
            P(("roll", "head"), None),
            P("roll", "head"),
            P("roll", "head"),
        ),
        check_vma=False,
    )
```

```python
import functools
import math

import jax
import jax.numpy as jnp
from jax import lax
from jax.experimental import pallas as pl
from jax.experimental.pallas import tpu as pltpu
from jax.sharding import PartitionSpec as P

HD = 128
BLOCK = 128
GROUP = 8
LIST = 4
QTOK = 256
NX = 4
NY = 4
NH = 8
WIDE = GROUP * HD
ROWS = QTOK // NH
KEYS = LIST * BLOCK + QTOK
NONE = KEYS // BLOCK
PAIR = 2 * HD
STEPS = GROUP // 2
CUTS = (2, 3, 4, 4)
LAG = 1
VMEM_MIB = 56
FIRST = 1
TOGETHER = 3
ORDER_OUT = (1, 2, 3, 4, 5, 6, 7)
MESH = pl.DeviceIdType.MESH
SCALE = 1.0 / math.sqrt(HD)
LOG2E = math.log2(math.e)
F32 = jnp.float32
BF16 = jnp.bfloat16


def roll_of(x, y, z):
    return (y * 2 + z) * NX + x


def dot(a, b, ca, cb):
    return lax.dot_general(a, b, (((ca,), (cb,)), ((), ())), preferred_element_type=F32)


def kernel(
    q_ref, g_ref, k_ref, v_ref, dk_ref, dv_ref, cite_hbm, list_hbm,
    att_ref, qg_ref, kg_ref, vg_ref, dkg_ref, dvg_ref,
    qw, gw, kw, vw, ag, sel, pool, cat, cat_t, acc, att, dq, kv_out, gs, gr, s1, r1, zs, zr,
    open_sem, cite_v_ref, cite_ref, list_ref, small_sem, par_v, par_ref, pos_ref, par_sem, own_q, own_doc, kv_s, kv_r, head_s, head_r, z_s, z_r, one_s, one_r, two_s, two_r,
    kvo_s, kvo_r, out_s, out_r, out_l, two_bs, two_br, one_bs, one_br, zb_s, zb_r,
):
    roll = lax.axis_index("roll")
    head = lax.axis_index("head")
    x = lax.rem(roll, NX)
    zh = lax.rem(roll // NX, 2)
    y = roll // (2 * NX)
    z_dev = (roll_of(x, y, 1 - zh), head)

    place = (x, y)
    size = (NX, NY)
    docs = (dk_ref, dv_ref)

    def at(t, a, b, z):
        return roll_of(a, b, z) if t == 0 else roll_of(b, a, z)

    def first(t, d):
        a = lax.rem(place[t] + d, size[t])
        return (at(t, a, place[1 - t], zh), head)

    def second(t, d):
        b = lax.rem(place[1 - t] + d, size[1 - t])
        return (at(t, place[t], b, zh), head)

    def remote(src, dst, ss, rs, dev):
        return pltpu.make_async_remote_copy(
            src_ref=src, dst_ref=dst, send_sem=ss, recv_sem=rs, device_id=dev, device_id_type=MESH
        )

    def landed(ref, sem):
        pltpu.make_async_copy(ref, ref, sem).wait()

    barrier = pltpu.get_barrier_semaphore()
    partners = [first(t, d) for t in range(2) for d in range(1, size[t])]
    partners += [(roll, lax.rem(head + k, NH)) for k in range(1, NH)]
    for dev in partners:
        pl.semaphore_signal(barrier, inc=1, device_id=dev, device_id_type=MESH)
    small = [
        pltpu.make_async_copy(cite_hbm, cite_v_ref, small_sem.at[0]),
        pltpu.make_async_copy(cite_hbm, cite_ref, small_sem.at[1]),
        pltpu.make_async_copy(list_hbm, list_ref, small_sem.at[2]),
    ]
    for c in small:
        c.start()
    gate, other_gate = (NH - 1) * (1 - zh), (NH - 1) * zh
    pl.semaphore_signal(
        barrier, inc=1, device_id=(roll_of(x, y, 1 - zh), other_gate), device_id_type=MESH
    )

    @pl.when(head == gate)
    def _():
        pl.semaphore_wait(barrier, len(partners) + NH)
        for k in range(1, NH):
            pl.semaphore_signal(
                open_sem, inc=1, device_id=(roll, lax.rem(head + k, NH)), device_id_type=MESH
            )

    @pl.when(head != gate)
    def _():
        pl.semaphore_wait(barrier, len(partners))

    for t in range(2):
        for d in range(1, size[t]):
            c = remote(
                docs[t], ag.at[t, 0, place[t]], one_s.at[t, 0], one_r.at[t, 0], first(t, d)
            )
            c.start()
    own_docs = []
    for t in range(2):
        c = pltpu.make_async_copy(docs[t], ag.at[t, 0, place[t]], own_doc.at[t])
        c.start()
        own_docs.append(c)
    half = head // (NH // 2)
    heads = []
    mine = pl.ds(pl.multiple_of(head * ROWS, ROWS), ROWS)
    moved = ((k_ref, kw, HD), (v_ref, vw, HD), (q_ref, qw, WIDE), (g_ref, gw, WIDE))
    for i, (src, dst, width) in enumerate(moved):
        c = pltpu.make_async_copy(
            src.at[:, pl.ds(pl.multiple_of(head * width, width), width)], dst.at[mine], own_q.at[i]
        )
        c.start()
        heads.append(c)

    def kv_copy(k, i):
        h = lax.rem(head + k, NH)
        src, dst, width = moved[i]
        return remote(
            src.at[:, pl.ds(pl.multiple_of(h * width, width), width)],
            dst.at[mine], kv_s.at[i], kv_r.at[i], (roll, h),
        )

    def chunk_copy(k, i, j):
        h = lax.rem(head + k, NH)
        src, dst, width = moved[2 + i]
        return remote(
            src.at[:, pl.ds(pl.multiple_of(h * width + j * PAIR, PAIR), PAIR)],
            dst.at[mine, pl.ds(pl.multiple_of(j * PAIR, PAIR), PAIR)],
            head_s.at[i], head_r.at[i, j, half], (roll, h),
        )

    for k in range(1, NH):
        for i in range(2):
            kv_copy(k, i).start()

    def send_chunks(j, _):
        for k in range(1, NH):
            for i in range(2):
                chunk_copy(k, i, j).start()
        return 0

    lax.fori_loop(0, FIRST, send_chunks, 0)

    @pl.when(head != gate)
    def _():
        pl.semaphore_wait(open_sem, 1)

    z_copy = []
    for t in range(2):
        c = remote(docs[t], ag.at[t, 1, place[t]], z_s.at[t], z_r.at[t], z_dev)
        c.start()
        z_copy.append(c)
    lax.fori_loop(FIRST, STEPS, send_chunks, 0)

    for c in small:
        c.wait()
    cites = cite_v_ref[...]
    rolls = 2 * NX * NY
    owner_at = lax.broadcasted_iota(jnp.int32, (rolls, rolls), 0)
    odd = jnp.zeros((rolls, rolls), jnp.int32)
    for c in range(cites.shape[0]):
        cite = cites[c : c + 1]
        odd = odd + jnp.where((cite >> 1) == owner_at, cite & 1, 0)

    par_v[:, 0:rolls] = odd.astype(F32)
    par_copy = pltpu.make_async_copy(par_v, par_ref, par_sem.at[0])
    par_copy.start()
    acc[...] = jnp.zeros_like(acc)
    par_copy.wait()

    owners = [[cite_ref[list_ref[b, i], roll] >> 1 for i in range(LIST)] for b in range(2)]

    def find(o, _):
        for b in range(2):
            found = jnp.int32(NONE)
            for i in range(LIST):
                same = (owners[b][i] == o).astype(jnp.int32)
                found = found + same * (i - found)
            pos_ref[b, o] = found
        return 0

    lax.fori_loop(0, rolls, find, 0)

    def slot(t, p, b, a):
        return (p * size[1 - t] + b) * size[t] + a

    def pick(t, p):
        o_z = zh if p == 0 else 1 - zh
        for d in range(size[1 - t]):
            target = second(t, d)[0]

            def step(a, _):
                pr = par_ref[at(t, a, place[1 - t], o_z), target]
                low = ag[t, p, a, 0:BLOCK].astype(F32)
                high = ag[t, p, a, BLOCK : 2 * BLOCK].astype(F32)
                chosen = (low * (1.0 - pr) + high * pr).astype(BF16)
                if d == 0:
                    pool[t, slot(t, p, place[1 - t], a)] = chosen
                else:
                    sel[t, p, d - 1, a] = chosen
                return 0

            lax.fori_loop(0, size[t], step, 0)

    for p in range(2):
        if p == 1:
            for t in range(2):
                z_copy[t].wait_recv()
                for d in range(1, size[t]):
                    c = remote(
                        ag.at[t, 1, place[t]], ag.at[t, 1, place[t]],
                        one_s.at[t, 1], one_r.at[t, 1], first(t, d),
                    )
                    c.start()
        for t in range(2):
            if p == 0:
                own_docs[t].wait()
            landed(ag.at[t, p, 0 : size[t] - 1], one_r.at[t, p])
            pick(t, p)
            for d in range(1, size[1 - t]):
                c = remote(
                    sel.at[t, p, d - 1], pool.at[t, pl.ds(slot(t, p, place[1 - t], 0), size[t])],
                    two_s.at[t, p], two_r.at[t, p], second(t, d),
                )
                c.start()
    for c in heads:
        c.wait()
    others = QTOK - ROWS
    for i, ref in enumerate((kw, vw)):
        landed(ref.at[0:others], kv_r.at[i])
    for t in range(2):
        for p in range(2):
            landed(pool.at[t, 0 : (size[1 - t] - 1) * size[t]], two_r.at[t, p])

    for b in range(2):
        for i in range(LIST):
            o = owners[b][i]
            ox, oz, oy = o & (NX - 1), (o // NX) & 1, o // (2 * NX)
            slots = [((oz ^ zh) * NY + oy) * NX + ox, ((oz ^ zh) * NX + ox) * NY + oy]
            rows = pl.ds(i * BLOCK, BLOCK)
            for t in range(2):
                cat[t, b, rows] = pool[t, slots[t]]
        cat[0, b, LIST * BLOCK : KEYS] = kw[...]
        cat[1, b, LIST * BLOCK : KEYS] = vw[...]
        for t in range(2):
            cat_t[t, b] = cat[t, b].T

    def compute(b, j):
        c0 = pl.multiple_of(j * PAIR, PAIR)
        c1 = pl.multiple_of(c0 + HD, HD)
        rows = pl.ds(pl.multiple_of(b * BLOCK, BLOCK), BLOCK)
        cols = (pl.ds(c0, HD), pl.ds(c1, HD))
        query = jnp.concatenate([qw[rows, c] for c in cols], axis=0)
        grad = jnp.concatenate([gw[rows, c] for c in cols], axis=0)
        score = dot(cat[0, b], query, 1, 1)
        local = score[LIST * BLOCK :]
        key_at = lax.broadcasted_iota(jnp.int32, local.shape, 0)
        query_at = lax.rem(lax.broadcasted_iota(jnp.int32, local.shape, 1), BLOCK) + b * BLOCK
        local = jnp.where(key_at <= query_at, local, -jnp.inf)
        score = jnp.concatenate([score[: LIST * BLOCK], local], axis=0)
        top = jnp.max(score, axis=0, keepdims=True)
        e = jnp.exp2((score - top) * (SCALE * LOG2E))
        prob = e * (1.0 / jnp.sum(e, axis=0, keepdims=True))
        weight = prob.astype(BF16)
        dprob = dot(cat[1, b], grad, 1, 1)
        delta = jnp.sum(prob * dprob, axis=0, keepdims=True)
        dscore = (prob * (dprob - delta)).astype(BF16)
        acc[1, b, 0:NONE] += dot(weight, grad, 1, 0).reshape(NONE, BLOCK, HD)
        acc[0, b, 0:NONE] += dot(dscore, query, 1, 0).reshape(NONE, BLOCK, HD)
        out_t = dot(cat_t[1, b], weight, 1, 0)
        dq_t = dot(cat_t[0, b], dscore, 1, 0) * SCALE
        for i, c in enumerate(cols):
            att[rows, c] = out_t[:, i * HD : (i + 1) * HD].T.astype(BF16)
            dq[rows, c] = dq_t[:, i * HD : (i + 1) * HD].T.astype(BF16)

    back = ((att, att_ref, WIDE), (dq, qg_ref, WIDE), (kv_out.at[0], kg_ref, HD), (kv_out.at[1], vg_ref, HD))

    def own_out(i):
        src, dst, width = back[i]
        there = pl.ds(pl.multiple_of(head * width, width), width)
        return pltpu.make_async_copy(src.at[mine], dst.at[:, there], out_l.at[i])

    def kv_back(k, i):
        h = lax.rem(head + k, NH)
        src, dst, width = back[2 + i]
        theirs = pl.ds(pl.multiple_of(h * ROWS, ROWS), ROWS)
        there = pl.ds(pl.multiple_of(head * width, width), width)
        return remote(src.at[theirs], dst.at[:, there], kvo_s.at[i], kvo_r.at[i], (roll, h))

    def chunk_back(k, i, j):
        h = lax.rem(head + k, NH)
        src, dst, width = back[i]
        theirs = pl.ds(pl.multiple_of(h * ROWS, ROWS), ROWS)
        return remote(
            src.at[theirs, pl.ds(pl.multiple_of(j * PAIR, PAIR), PAIR)],
            dst.at[:, pl.ds(pl.multiple_of(head * width + j * PAIR, PAIR), PAIR)],
            out_s.at[i], out_r.at[i], (roll, h),
        )

    def send_back(j, _):
        for k in ORDER_OUT:
            for i in range(2):
                chunk_back(k, i, j).start()
        return 0

    def wait_half(j, side):
        rows = QTOK // 2 if side else QTOK // 2 - ROWS
        cols = pl.ds(pl.multiple_of(j * PAIR, PAIR), PAIR)
        for i, ref in enumerate((qw, gw)):
            landed(ref.at[0:rows, cols], head_r.at[i, j, half if side == 0 else 1 - half])

    def per_chunk(j, _):
        wait_half(j, 0)
        wait_half(j, 1)
        compute(0, j)
        compute(1, j)
        after_chunk(j)
        return 0

    def per_half(j, _):
        def step(side, _):
            @pl.when(side == 0)
            def _():
                wait_half(j, 0)

            @pl.when(side == 1)
            def _():
                wait_half(j, 1)

            compute(half ^ side, j)
            return 0

        lax.fori_loop(0, 2, step, 0)
        after_chunk(j)
        return 0

    def after_chunk(j):
        @pl.when((j >= LAG) & (j < CUTS[0] + LAG))
        def _():
            send_back(j - LAG, 0)

    lax.fori_loop(0, TOGETHER, per_chunk, 0)
    lax.fori_loop(TOGETHER, STEPS, per_half, 0)

    def prepare(t, p, b):
        def step(a, _):
            o = at(t, a, b, zh if p == 0 else 1 - zh)
            total = acc[t, 0, pos_ref[0, o]] + acc[t, 1, pos_ref[1, o]]
            if t == 0:
                total = total * SCALE
            gs[t, p, b, a] = total.astype(BF16)

        for a in range(size[t]):
            step(a, 0)

    def send_two(p):
        for d in range(1, NX):
            for t in range(2):
                b = lax.rem(place[1 - t] + d, size[1 - t])
                prepare(t, p, b)
                c = remote(
                    gs.at[t, p, b], gr.at[t, p, place[1 - t]],
                    two_bs.at[t, p], two_br.at[t, p], second(t, d),
                )
                c.start()

    def own_two(p):
        for t in range(2):
            b = place[1 - t]
            prepare(t, p, b)
            gr[t, p, b] = gs[t, p, b]

    send_two(1)
    send_two(0)
    lax.fori_loop(CUTS[0], CUTS[1], send_back, 0)
    own_two(1)
    own_two(0)

    for t in range(2):
        total = (acc[t, 0, LIST:NONE] + acc[t, 1, LIST:NONE]).reshape(QTOK, HD)
        if t == 0:
            total = total * SCALE
        kv_out[t] = total.astype(BF16)

    for i in range(4):
        own_out(i).start()
    for k in range(1, NH):
        for i in range(2):
            kv_back(k, i).start()

    back_z = []

    def merge_rolls(t, p):
        o_z = zh if p == 0 else 1 - zh

        def merge(a, _):
            o = at(t, a, place[1 - t], o_z)
            low = high = jnp.zeros((BLOCK, HD), F32)
            for b in range(size[1 - t]):
                pr = par_ref[o, at(t, place[t], b, zh)]
                m = gr[t, p, b, a].astype(F32)
                low = low + m * (1.0 - pr)
                high = high + m * pr
            s1[t, p, a, 0:BLOCK] = low.astype(BF16)
            s1[t, p, a, BLOCK : 2 * BLOCK] = high.astype(BF16)
            return 0

        lax.fori_loop(0, size[t], merge, 0)

    for p in (1, 0):
        if p == 0:
            lax.fori_loop(CUTS[2], CUTS[3], send_back, 0)
            for c in z_copy:
                c.wait_send()
            for i, ref in enumerate((kw, vw)):
                landed(ref.at[0:others], kv_s.at[i])
            for i, ref in enumerate((qw, gw)):
                landed(ref.at[0:others], head_s.at[i])
            for t in range(2):
                for q in range(2):
                    landed(ag.at[t, q, 0 : size[t] - 1], one_s.at[t, q])
                    landed(sel.at[t, q], two_s.at[t, q])
                landed(gs.at[t, 1, 0 : size[1 - t] - 1], two_bs.at[t, 1])
            for i in range(4):
                own_out(i).wait()
        for t in range(2):
            landed(gr.at[t, p, 0 : size[1 - t] - 1], two_br.at[t, p])
            merge_rolls(t, p)
            for d in range(1, size[t]):
                a = lax.rem(place[t] + d, size[t])
                c = remote(
                    s1.at[t, p, a], r1.at[t, p, place[t]],
                    one_bs.at[t, p], one_br.at[t, p], first(t, d),
                )
                c.start()
            r1[t, p, place[t]] = s1[t, p, place[t]]
        if p == 1:
            lax.fori_loop(CUTS[1], CUTS[2], send_back, 0)
        for t in range(2):
            landed(r1.at[t, p, 0 : size[t] - 1], one_br.at[t, p])
            total = r1[t, p, 0].astype(F32)
            for a in range(1, size[t]):
                total = total + r1[t, p, a].astype(F32)
            if p == 1:
                zs[t] = total.astype(BF16)
                c = remote(zs.at[t], zr.at[t], zb_s.at[t], zb_r.at[t], z_dev)
                c.start()
                back_z.append(c)
            else:
                if t == 0:
                    lax.fori_loop(CUTS[3], STEPS, send_back, 0)
                    for i in range(2):
                        for u in range(2):
                            landed(r1.at[u, i, 0 : size[u] - 1], one_bs.at[u, i])
                        landed(gs.at[i, 0, 0 : size[1 - i] - 1], two_bs.at[i, 0])
                        landed(kg_ref.at[:, 0 : HD * (NH - 1)], kvo_r.at[i])
                        landed(kv_out.at[i, 0:others], kvo_s.at[i])
                        landed(att.at[0:others], out_s.at[i])
                back_z[t].wait_recv()
                (dkg_ref, dvg_ref)[t][...] = total + zr[t].astype(F32)

    for i in range(2):
        landed(att_ref.at[:, 0 : WIDE * (NH - 1)], out_r.at[i])
    for c in back_z:
        c.wait_send()


def copy_out(*refs):
    n = len(refs) // 2
    copies = [pltpu.make_async_copy(refs[i], refs[n + i], refs[-1].at[i]) for i in range(n)]
    for c in copies:
        c.start()
    for c in copies:
        c.wait()


def local(queries, keys, values, cotangent, doc_keys, doc_values, citations, block_lists):
    n = max(NX, NY)
    any_spec = pl.BlockSpec(memory_space=pltpu.HBM)
    vmem = pl.BlockSpec(memory_space=pltpu.VMEM)
    dma = pltpu.SemaphoreType.DMA
    blk = (BLOCK, HD)
    sd = jax.ShapeDtypeStruct
    results = pl.pallas_call(
        kernel,
        out_shape=(
            pltpu.VMEM(queries.shape, BF16), pltpu.VMEM(queries.shape, BF16),
            pltpu.VMEM(keys.shape, BF16), pltpu.VMEM(keys.shape, BF16),
            pltpu.VMEM(doc_keys.shape, F32), pltpu.VMEM(doc_keys.shape, F32),
        ),
        in_specs=[any_spec] * 8,
        out_specs=(vmem,) * 6,
        scratch_shapes=[
            pltpu.VMEM((QTOK, WIDE), BF16),
            pltpu.VMEM((QTOK, WIDE), BF16),
            pltpu.VMEM((QTOK, HD), BF16),
            pltpu.VMEM((QTOK, HD), BF16),
            pltpu.VMEM((2, 2, n, 2 * BLOCK, HD), BF16),
            pltpu.VMEM((2, 2, n - 1, n) + blk, BF16),
            pltpu.VMEM((2, 2 * n * n) + blk, BF16),
            pltpu.VMEM((2, 2, KEYS, HD), BF16),
            pltpu.VMEM((2, 2, HD, KEYS), BF16),
            pltpu.VMEM((2, 2, NONE + 1) + blk, F32),
            pltpu.VMEM((QTOK, WIDE), BF16),
            pltpu.VMEM((QTOK, WIDE), BF16),
            pltpu.VMEM((2, QTOK, HD), BF16),
            pltpu.VMEM((2, 2, n, n) + blk, BF16),
            pltpu.VMEM((2, 2, n, n) + blk, BF16),
            pltpu.VMEM((2, 2, n, 2 * BLOCK, HD), BF16),
            pltpu.VMEM((2, 2, n, 2 * BLOCK, HD), BF16),
            pltpu.VMEM((2, 2 * BLOCK, HD), BF16),
            pltpu.VMEM((2, 2 * BLOCK, HD), BF16),
            pltpu.SemaphoreType.REGULAR,
            pltpu.VMEM(citations.shape[::-1], jnp.int32),
            pltpu.SMEM(citations.shape[::-1], jnp.int32),
            pltpu.SMEM(block_lists.shape, jnp.int32),
            dma((3,)),
            pltpu.VMEM((2 * NX * NY, HD), F32),
            pltpu.SMEM((2 * NX * NY, HD), F32),
            pltpu.SMEM((2, 2 * NX * NY), jnp.int32),
            dma((1,)),
            dma((4,)), dma((2,)), dma((2,)), dma((2,)), dma((2,)), dma((2, STEPS, 2)),
            dma((2,)), dma((2,)),
            dma((2, 2)), dma((2, 2)), dma((2, 2)), dma((2, 2)),
            dma((2,)), dma((2,)), dma((2,)), dma((2,)), dma((4,)),
            dma((2, 2)), dma((2, 2)), dma((2, 2)), dma((2, 2)), dma((2,)), dma((2,)),
        ],
        compiler_params=pltpu.CompilerParams(
            collective_id=0, has_side_effects=True, vmem_limit_bytes=VMEM_MIB * 2**20
        ),
        name="attention",
    )(*[pltpu.with_memory_space_constraint(r, pltpu.HBM) for r in (queries, cotangent, keys, values, doc_keys, doc_values, citations.T, block_lists)])
    return pl.pallas_call(
        copy_out,
        out_shape=tuple(sd(r.shape, r.dtype) for r in results),
        in_specs=[vmem] * 6,
        out_specs=(any_spec,) * 6,
        scratch_shapes=[dma((6,))],
        compiler_params=pltpu.CompilerParams(vmem_limit_bytes=VMEM_MIB * 2**20),
        name="copy_out",
    )(*[pltpu.with_memory_space_constraint(r, pltpu.VMEM) for r in results])


def solution(mesh):
    return jax.shard_map(
        local,
        mesh=mesh,
        in_specs=(
            P(("roll", "head"), None),
            P(("roll", "head"), None),
            P(("roll", "head"), None),
            P(("roll", "head"), None),
            P("roll", "head"),
            P("roll", "head"),
            P(),
            P("roll", None),
        ),
        out_specs=(
            P(("roll", "head"), None),
            P(("roll", "head"), None),
            P(("roll", "head"), None),
            P(("roll", "head"), None),
            P("roll", "head"),
            P("roll", "head"),
        ),
        check_vma=False,
    )
```

```python
import functools
import math

import jax
import jax.numpy as jnp
from jax import lax
from jax.experimental import pallas as pl
from jax.experimental.pallas import tpu as pltpu
from jax.sharding import PartitionSpec as P

HD = 128
BLOCK = 128
GROUP = 8
LIST = 4
QTOK = 256
NX = 4
NY = 4
NH = 8
WIDE = GROUP * HD
ROWS = QTOK // NH
KEYS = LIST * BLOCK + QTOK
NONE = KEYS // BLOCK
PAIR = 2 * HD
STEPS = GROUP // 2
CUTS = (2, 3, 4, 4)
LAG = 1
VMEM_MIB = 56
FIRST = 1
TOGETHER = 2
ORDER_IN = (4, 3, 5, 2, 6, 1, 7)
ORDER_OUT = (1, 2, 3, 4, 5, 6, 7)
MESH = pl.DeviceIdType.MESH
SCALE = 1.0 / math.sqrt(HD)
LOG2E = math.log2(math.e)
F32 = jnp.float32
BF16 = jnp.bfloat16


def roll_of(x, y, z):
    return (y * 2 + z) * NX + x


def dot(a, b, ca, cb):
    return lax.dot_general(a, b, (((ca,), (cb,)), ((), ())), preferred_element_type=F32)


def kernel(
    q_ref, g_ref, k_ref, v_ref, dk_ref, dv_ref, cite_hbm, list_hbm,
    att_ref, qg_ref, kg_ref, vg_ref, dkg_ref, dvg_ref,
    qw, gw, kw, vw, ag, sel, pool, cat, cat_t, acc, att, dq, kv_out, gs, gr, s1, r1, zs, zr,
    open_sem, cite_v_ref, cite_ref, list_ref, small_sem, par_v, par_ref, pos_ref, par_sem, own_q, own_doc, kv_s, kv_r, head_s, head_r, z_s, z_r, one_s, one_r, two_s, two_r,
    kvo_s, kvo_r, out_s, out_r, out_l, two_bs, two_br, one_bs, one_br, zb_s, zb_r,
):
    roll = lax.axis_index("roll")
    head = lax.axis_index("head")
    x = lax.rem(roll, NX)
    zh = lax.rem(roll // NX, 2)
    y = roll // (2 * NX)
    z_dev = (roll_of(x, y, 1 - zh), head)

    place = (x, y)
    size = (NX, NY)
    docs = (dk_ref, dv_ref)

    def at(t, a, b, z):
        return roll_of(a, b, z) if t == 0 else roll_of(b, a, z)

    def first(t, d):
        a = lax.rem(place[t] + d, size[t])
        return (at(t, a, place[1 - t], zh), head)

    def second(t, d):
        b = lax.rem(place[1 - t] + d, size[1 - t])
        return (at(t, place[t], b, zh), head)

    def remote(src, dst, ss, rs, dev):
        return pltpu.make_async_remote_copy(
            src_ref=src, dst_ref=dst, send_sem=ss, recv_sem=rs, device_id=dev, device_id_type=MESH
        )

    def landed(ref, sem):
        pltpu.make_async_copy(ref, ref, sem).wait()

    barrier = pltpu.get_barrier_semaphore()
    partners = [first(t, d) for t in range(2) for d in range(1, size[t])]
    partners += [(roll, lax.rem(head + k, NH)) for k in range(1, NH)]
    for dev in partners:
        pl.semaphore_signal(barrier, inc=1, device_id=dev, device_id_type=MESH)
    small = [
        pltpu.make_async_copy(cite_hbm, cite_v_ref, small_sem.at[0]),
        pltpu.make_async_copy(cite_hbm, cite_ref, small_sem.at[1]),
        pltpu.make_async_copy(list_hbm, list_ref, small_sem.at[2]),
    ]
    for c in small:
        c.start()
    gate, other_gate = (NH - 1) * (1 - zh), (NH - 1) * zh
    pl.semaphore_signal(
        barrier, inc=1, device_id=(roll_of(x, y, 1 - zh), other_gate), device_id_type=MESH
    )

    @pl.when(head == gate)
    def _():
        pl.semaphore_wait(barrier, len(partners) + NH)
        for k in range(1, NH):
            pl.semaphore_signal(
                open_sem, inc=1, device_id=(roll, lax.rem(head + k, NH)), device_id_type=MESH
            )

    @pl.when(head != gate)
    def _():
        pl.semaphore_wait(barrier, len(partners))

    for t in range(2):
        for d in range(1, size[t]):
            c = remote(
                docs[t], ag.at[t, 0, place[t]], one_s.at[t, 0], one_r.at[t, 0], first(t, d)
            )
            c.start()
    own_docs = []
    for t in range(2):
        c = pltpu.make_async_copy(docs[t], ag.at[t, 0, place[t]], own_doc.at[t])
        c.start()
        own_docs.append(c)
    half = head // (NH // 2)
    heads = []
    mine = pl.ds(pl.multiple_of(head * ROWS, ROWS), ROWS)
    moved = ((k_ref, kw, HD), (v_ref, vw, HD), (q_ref, qw, WIDE), (g_ref, gw, WIDE))
    for i, (src, dst, width) in enumerate(moved):
        c = pltpu.make_async_copy(
            src.at[:, pl.ds(pl.multiple_of(head * width, width), width)], dst.at[mine], own_q.at[i]
        )
        c.start()
        heads.append(c)

    def kv_copy(k, i):
        h = lax.rem(head + k, NH)
        src, dst, width = moved[i]
        return remote(
            src.at[:, pl.ds(pl.multiple_of(h * width, width), width)],
            dst.at[mine], kv_s.at[i], kv_r.at[i], (roll, h),
        )

    def chunk_copy(k, i, j):
        h = lax.rem(head + k, NH)
        src, dst, width = moved[2 + i]
        return remote(
            src.at[:, pl.ds(pl.multiple_of(h * width + j * PAIR, PAIR), PAIR)],
            dst.at[mine, pl.ds(pl.multiple_of(j * PAIR, PAIR), PAIR)],
            head_s.at[i], head_r.at[i, j, half], (roll, h),
        )

    for k in range(1, NH):
        for i in range(2):
            kv_copy(k, i).start()

    def send_chunks(j, _):
        for k in ORDER_IN:
            for i in range(2):
                chunk_copy(k, i, j).start()
        return 0

    lax.fori_loop(0, FIRST, send_chunks, 0)

    @pl.when(head != gate)
    def _():
        pl.semaphore_wait(open_sem, 1)

    z_copy = []
    for t in range(2):
        c = remote(docs[t], ag.at[t, 1, place[t]], z_s.at[t], z_r.at[t], z_dev)
        c.start()
        z_copy.append(c)
    lax.fori_loop(FIRST, STEPS, send_chunks, 0)

    for c in small:
        c.wait()
    cites = cite_v_ref[...]
    rolls = 2 * NX * NY
    owner_at = lax.broadcasted_iota(jnp.int32, (rolls, rolls), 0)
    odd = jnp.zeros((rolls, rolls), jnp.int32)
    for c in range(cites.shape[0]):
        cite = cites[c : c + 1]
        odd = odd + jnp.where((cite >> 1) == owner_at, cite & 1, 0)

    par_v[:, 0:rolls] = odd.astype(F32)
    par_copy = pltpu.make_async_copy(par_v, par_ref, par_sem.at[0])
    par_copy.start()
    acc[...] = jnp.zeros_like(acc)
    par_copy.wait()

    owners = [[cite_ref[list_ref[b, i], roll] >> 1 for i in range(LIST)] for b in range(2)]

    def find(o, _):
        for b in range(2):
            found = jnp.int32(NONE)
            for i in range(LIST):
                same = (owners[b][i] == o).astype(jnp.int32)
                found = found + same * (i - found)
            pos_ref[b, o] = found
        return 0

    lax.fori_loop(0, rolls, find, 0)

    def slot(t, p, b, a):
        return (p * size[1 - t] + b) * size[t] + a

    def pick(t, p):
        o_z = zh if p == 0 else 1 - zh
        for d in range(size[1 - t]):
            target = second(t, d)[0]

            def step(a, _):
                pr = par_ref[at(t, a, place[1 - t], o_z), target]
                low = ag[t, p, a, 0:BLOCK].astype(F32)
                high = ag[t, p, a, BLOCK : 2 * BLOCK].astype(F32)
                chosen = (low * (1.0 - pr) + high * pr).astype(BF16)
                if d == 0:
                    pool[t, slot(t, p, place[1 - t], a)] = chosen
                else:
                    sel[t, p, d - 1, a] = chosen
                return 0

            lax.fori_loop(0, size[t], step, 0)

    for p in range(2):
        if p == 1:
            for t in range(2):
                z_copy[t].wait_recv()
                for d in range(1, size[t]):
                    c = remote(
                        ag.at[t, 1, place[t]], ag.at[t, 1, place[t]],
                        one_s.at[t, 1], one_r.at[t, 1], first(t, d),
                    )
                    c.start()
        for t in range(2):
            if p == 0:
                own_docs[t].wait()
            landed(ag.at[t, p, 0 : size[t] - 1], one_r.at[t, p])
            pick(t, p)
            for d in range(1, size[1 - t]):
                c = remote(
                    sel.at[t, p, d - 1], pool.at[t, pl.ds(slot(t, p, place[1 - t], 0), size[t])],
                    two_s.at[t, p], two_r.at[t, p], second(t, d),
                )
                c.start()
    for c in heads:
        c.wait()
    others = QTOK - ROWS
    for i, ref in enumerate((kw, vw)):
        landed(ref.at[0:others], kv_r.at[i])
    for t in range(2):
        for p in range(2):
            landed(pool.at[t, 0 : (size[1 - t] - 1) * size[t]], two_r.at[t, p])

    for b in range(2):
        for i in range(LIST):
            o = owners[b][i]
            ox, oz, oy = o & (NX - 1), (o // NX) & 1, o // (2 * NX)
            slots = [((oz ^ zh) * NY + oy) * NX + ox, ((oz ^ zh) * NX + ox) * NY + oy]
            rows = pl.ds(i * BLOCK, BLOCK)
            for t in range(2):
                cat[t, b, rows] = pool[t, slots[t]]
        cat[0, b, LIST * BLOCK : KEYS] = kw[...]
        cat[1, b, LIST * BLOCK : KEYS] = vw[...]
        for t in range(2):
            cat_t[t, b] = cat[t, b].T

    def compute(b, j):
        c0 = pl.multiple_of(j * PAIR, PAIR)
        c1 = pl.multiple_of(c0 + HD, HD)
        rows = pl.ds(pl.multiple_of(b * BLOCK, BLOCK), BLOCK)
        cols = (pl.ds(c0, HD), pl.ds(c1, HD))
        query = jnp.concatenate([qw[rows, c] for c in cols], axis=0)
        grad = jnp.concatenate([gw[rows, c] for c in cols], axis=0)
        score = dot(cat[0, b], query, 1, 1)
        local = score[LIST * BLOCK :]
        key_at = lax.broadcasted_iota(jnp.int32, local.shape, 0)
        query_at = lax.rem(lax.broadcasted_iota(jnp.int32, local.shape, 1), BLOCK) + b * BLOCK
        local = jnp.where(key_at <= query_at, local, -jnp.inf)
        score = jnp.concatenate([score[: LIST * BLOCK], local], axis=0)
        top = jnp.max(score, axis=0, keepdims=True)
        e = jnp.exp2((score - top) * (SCALE * LOG2E))
        prob = e * (1.0 / jnp.sum(e, axis=0, keepdims=True))
        weight = prob.astype(BF16)
        dprob = dot(cat[1, b], grad, 1, 1)
        delta = jnp.sum(prob * dprob, axis=0, keepdims=True)
        dscore = (prob * (dprob - delta)).astype(BF16)
        acc[1, b, 0:NONE] += dot(weight, grad, 1, 0).reshape(NONE, BLOCK, HD)
        acc[0, b, 0:NONE] += dot(dscore, query, 1, 0).reshape(NONE, BLOCK, HD)
        out_t = dot(cat_t[1, b], weight, 1, 0)
        dq_t = dot(cat_t[0, b], dscore, 1, 0) * SCALE
        for i, c in enumerate(cols):
            att[rows, c] = out_t[:, i * HD : (i + 1) * HD].T.astype(BF16)
            dq[rows, c] = dq_t[:, i * HD : (i + 1) * HD].T.astype(BF16)

    back = ((att, att_ref, WIDE), (dq, qg_ref, WIDE), (kv_out.at[0], kg_ref, HD), (kv_out.at[1], vg_ref, HD))

    def own_out(i):
        src, dst, width = back[i]
        there = pl.ds(pl.multiple_of(head * width, width), width)
        return pltpu.make_async_copy(src.at[mine], dst.at[:, there], out_l.at[i])

    def kv_back(k, i):
        h = lax.rem(head + k, NH)
        src, dst, width = back[2 + i]
        theirs = pl.ds(pl.multiple_of(h * ROWS, ROWS), ROWS)
        there = pl.ds(pl.multiple_of(head * width, width), width)
        return remote(src.at[theirs], dst.at[:, there], kvo_s.at[i], kvo_r.at[i], (roll, h))

    def chunk_back(k, i, j):
        h = lax.rem(head + k, NH)
        src, dst, width = back[i]
        theirs = pl.ds(pl.multiple_of(h * ROWS, ROWS), ROWS)
        return remote(
            src.at[theirs, pl.ds(pl.multiple_of(j * PAIR, PAIR), PAIR)],
            dst.at[:, pl.ds(pl.multiple_of(head * width + j * PAIR, PAIR), PAIR)],
            out_s.at[i], out_r.at[i], (roll, h),
        )

    def send_back(j, _):
        for k in ORDER_OUT:
            for i in range(2):
                chunk_back(k, i, j).start()
        return 0

    def wait_half(j, side):
        rows = QTOK // 2 if side else QTOK // 2 - ROWS
        cols = pl.ds(pl.multiple_of(j * PAIR, PAIR), PAIR)
        for i, ref in enumerate((qw, gw)):
            landed(ref.at[0:rows, cols], head_r.at[i, j, half if side == 0 else 1 - half])

    def per_chunk(j, _):
        wait_half(j, 0)
        wait_half(j, 1)
        compute(0, j)
        compute(1, j)
        after_chunk(j)
        return 0

    def per_half(j, _):
        for side in range(2):
            wait_half(j, side)
            compute(half ^ side, j)
        after_chunk(j)
        return 0

    def after_chunk(j):
        @pl.when((j >= LAG) & (j < CUTS[0] + LAG))
        def _():
            send_back(j - LAG, 0)

    lax.fori_loop(0, TOGETHER, per_chunk, 0)
    lax.fori_loop(TOGETHER, STEPS, per_half, 0)

    def prepare(t, p, b):
        def step(a, _):
            o = at(t, a, b, zh if p == 0 else 1 - zh)
            total = acc[t, 0, pos_ref[0, o]] + acc[t, 1, pos_ref[1, o]]
            if t == 0:
                total = total * SCALE
            gs[t, p, b, a] = total.astype(BF16)

        for a in range(size[t]):
            step(a, 0)

    def send_two(p):
        for d in range(1, NX):
            for t in range(2):
                b = lax.rem(place[1 - t] + d, size[1 - t])
                prepare(t, p, b)
                c = remote(
                    gs.at[t, p, b], gr.at[t, p, place[1 - t]],
                    two_bs.at[t, p], two_br.at[t, p], second(t, d),
                )
                c.start()

    def own_two(p):
        for t in range(2):
            b = place[1 - t]
            prepare(t, p, b)
            gr[t, p, b] = gs[t, p, b]

    send_two(1)
    send_two(0)
    lax.fori_loop(CUTS[0], CUTS[1], send_back, 0)
    own_two(1)
    own_two(0)

    for t in range(2):
        total = (acc[t, 0, LIST:NONE] + acc[t, 1, LIST:NONE]).reshape(QTOK, HD)
        if t == 0:
            total = total * SCALE
        kv_out[t] = total.astype(BF16)

    for i in range(4):
        own_out(i).start()
    for k in range(1, NH):
        for i in range(2):
            kv_back(k, i).start()

    back_z = []

    def merge_rolls(t, p):
        o_z = zh if p == 0 else 1 - zh

        def merge(a, _):
            o = at(t, a, place[1 - t], o_z)
            low = high = jnp.zeros((BLOCK, HD), F32)
            for b in range(size[1 - t]):
                pr = par_ref[o, at(t, place[t], b, zh)]
                m = gr[t, p, b, a].astype(F32)
                low = low + m * (1.0 - pr)
                high = high + m * pr
            s1[t, p, a, 0:BLOCK] = low.astype(BF16)
            s1[t, p, a, BLOCK : 2 * BLOCK] = high.astype(BF16)
            return 0

        lax.fori_loop(0, size[t], merge, 0)

    for p in (1, 0):
        if p == 0:
            lax.fori_loop(CUTS[2], CUTS[3], send_back, 0)
            for c in z_copy:
                c.wait_send()
            for i, ref in enumerate((kw, vw)):
                landed(ref.at[0:others], kv_s.at[i])
            for i, ref in enumerate((qw, gw)):
                landed(ref.at[0:others], head_s.at[i])
            for t in range(2):
                for q in range(2):
                    landed(ag.at[t, q, 0 : size[t] - 1], one_s.at[t, q])
                    landed(sel.at[t, q], two_s.at[t, q])
                landed(gs.at[t, 1, 0 : size[1 - t] - 1], two_bs.at[t, 1])
            for i in range(4):
                own_out(i).wait()
        for t in range(2):
            landed(gr.at[t, p, 0 : size[1 - t] - 1], two_br.at[t, p])
            merge_rolls(t, p)
            for d in range(1, size[t]):
                a = lax.rem(place[t] + d, size[t])
                c = remote(
                    s1.at[t, p, a], r1.at[t, p, place[t]],
                    one_bs.at[t, p], one_br.at[t, p], first(t, d),
                )
                c.start()
            r1[t, p, place[t]] = s1[t, p, place[t]]
        if p == 1:
            lax.fori_loop(CUTS[1], CUTS[2], send_back, 0)
        for t in range(2):
            landed(r1.at[t, p, 0 : size[t] - 1], one_br.at[t, p])
            total = r1[t, p, 0].astype(F32)
            for a in range(1, size[t]):
                total = total + r1[t, p, a].astype(F32)
            if p == 1:
                zs[t] = total.astype(BF16)
                c = remote(zs.at[t], zr.at[t], zb_s.at[t], zb_r.at[t], z_dev)
                c.start()
                back_z.append(c)
            else:
                if t == 0:
                    lax.fori_loop(CUTS[3], STEPS, send_back, 0)
                    for i in range(2):
                        for u in range(2):
                            landed(r1.at[u, i, 0 : size[u] - 1], one_bs.at[u, i])
                        landed(gs.at[i, 0, 0 : size[1 - i] - 1], two_bs.at[i, 0])
                        landed(kg_ref.at[:, 0 : HD * (NH - 1)], kvo_r.at[i])
                        landed(kv_out.at[i, 0:others], kvo_s.at[i])
                        landed(att.at[0:others], out_s.at[i])
                back_z[t].wait_recv()
                (dkg_ref, dvg_ref)[t][...] = total + zr[t].astype(F32)

    for i in range(2):
        landed(att_ref.at[:, 0 : WIDE * (NH - 1)], out_r.at[i])
    for c in back_z:
        c.wait_send()


def copy_out(*refs):
    n = len(refs) // 2
    copies = [pltpu.make_async_copy(refs[i], refs[n + i], refs[-1].at[i]) for i in range(n)]
    for c in copies:
        c.start()
    for c in copies:
        c.wait()


def local(queries, keys, values, cotangent, doc_keys, doc_values, citations, block_lists):
    n = max(NX, NY)
    any_spec = pl.BlockSpec(memory_space=pltpu.HBM)
    vmem = pl.BlockSpec(memory_space=pltpu.VMEM)
    dma = pltpu.SemaphoreType.DMA
    blk = (BLOCK, HD)
    sd = jax.ShapeDtypeStruct
    results = pl.pallas_call(
        kernel,
        out_shape=(
            pltpu.VMEM(queries.shape, BF16), pltpu.VMEM(queries.shape, BF16),
            pltpu.VMEM(keys.shape, BF16), pltpu.VMEM(keys.shape, BF16),
            pltpu.VMEM(doc_keys.shape, F32), pltpu.VMEM(doc_keys.shape, F32),
        ),
        in_specs=[any_spec] * 8,
        out_specs=(vmem,) * 6,
        scratch_shapes=[
            pltpu.VMEM((QTOK, WIDE), BF16),
            pltpu.VMEM((QTOK, WIDE), BF16),
            pltpu.VMEM((QTOK, HD), BF16),
            pltpu.VMEM((QTOK, HD), BF16),
            pltpu.VMEM((2, 2, n, 2 * BLOCK, HD), BF16),
            pltpu.VMEM((2, 2, n - 1, n) + blk, BF16),
            pltpu.VMEM((2, 2 * n * n) + blk, BF16),
            pltpu.VMEM((2, 2, KEYS, HD), BF16),
            pltpu.VMEM((2, 2, HD, KEYS), BF16),
            pltpu.VMEM((2, 2, NONE + 1) + blk, F32),
            pltpu.VMEM((QTOK, WIDE), BF16),
            pltpu.VMEM((QTOK, WIDE), BF16),
            pltpu.VMEM((2, QTOK, HD), BF16),
            pltpu.VMEM((2, 2, n, n) + blk, BF16),
            pltpu.VMEM((2, 2, n, n) + blk, BF16),
            pltpu.VMEM((2, 2, n, 2 * BLOCK, HD), BF16),
            pltpu.VMEM((2, 2, n, 2 * BLOCK, HD), BF16),
            pltpu.VMEM((2, 2 * BLOCK, HD), BF16),
            pltpu.VMEM((2, 2 * BLOCK, HD), BF16),
            pltpu.SemaphoreType.REGULAR,
            pltpu.VMEM(citations.shape[::-1], jnp.int32),
            pltpu.SMEM(citations.shape[::-1], jnp.int32),
            pltpu.SMEM(block_lists.shape, jnp.int32),
            dma((3,)),
            pltpu.VMEM((2 * NX * NY, HD), F32),
            pltpu.SMEM((2 * NX * NY, HD), F32),
            pltpu.SMEM((2, 2 * NX * NY), jnp.int32),
            dma((1,)),
            dma((4,)), dma((2,)), dma((2,)), dma((2,)), dma((2,)), dma((2, STEPS, 2)),
            dma((2,)), dma((2,)),
            dma((2, 2)), dma((2, 2)), dma((2, 2)), dma((2, 2)),
            dma((2,)), dma((2,)), dma((2,)), dma((2,)), dma((4,)),
            dma((2, 2)), dma((2, 2)), dma((2, 2)), dma((2, 2)), dma((2,)), dma((2,)),
        ],
        compiler_params=pltpu.CompilerParams(
            collective_id=0, has_side_effects=True, vmem_limit_bytes=VMEM_MIB * 2**20
        ),
        name="attention",
    )(*[pltpu.with_memory_space_constraint(r, pltpu.HBM) for r in (queries, cotangent, keys, values, doc_keys, doc_values, citations.T, block_lists)])
    return pl.pallas_call(
        copy_out,
        out_shape=tuple(sd(r.shape, r.dtype) for r in results),
        in_specs=[vmem] * 6,
        out_specs=(any_spec,) * 6,
        scratch_shapes=[dma((6,))],
        compiler_params=pltpu.CompilerParams(vmem_limit_bytes=VMEM_MIB * 2**20),
        name="copy_out",
    )(*[pltpu.with_memory_space_constraint(r, pltpu.VMEM) for r in results])


def solution(mesh):
    return jax.shard_map(
        local,
        mesh=mesh,
        in_specs=(
            P(("roll", "head"), None),
            P(("roll", "head"), None),
            P(("roll", "head"), None),
            P(("roll", "head"), None),
            P("roll", "head"),
            P("roll", "head"),
            P(),
            P("roll", None),
        ),
        out_specs=(
            P(("roll", "head"), None),
            P(("roll", "head"), None),
            P(("roll", "head"), None),
            P(("roll", "head"), None),
            P("roll", "head"),
            P("roll", "head"),
        ),
        check_vma=False,
    )
```
